32 devices in a mesh: seq: 8 (over z, x), head: 4 (over y, core).
Axes of the slice: x: 2, y: 2, z: 4, core: 2. Of those that a mesh axis runs over, the one named last changes fastest.
Arguments:
- queries: bfloat16 [1024, 2560], P('seq', 'head'), may hold values from -6 to 6
- keys: bfloat16 [1024, 2560], P('seq', 'head'), may hold values from -6 to 6
- values: bfloat16 [1024, 2560], P('seq', 'head'), may hold values from -6 to 6
- head_class: int32 [20], replicated, may hold values from 0 to 1, as said below
- window_lengths: int32 [8, 4], P('seq'), may hold values from 1 to 64, 128 in all within a row
- out_weight: bfloat16 [2560, 5120], P('seq', 'head'), may hold values from -0.125 to 0.125
Outputs:
- projected: bfloat16 [1024, 5120], P('seq', 'head')
The draws below stay inside these ranges and needn't reach their ends.
Inputs may be any that keep to these rules, and one draw needn't show every extreme that they name: `head_class`: each group of 5 consecutive heads holds 1 to 3 temporal heads, and some group holds exactly 3. `window_lengths`: the 4 lengths of each block sum to 128, and the longest is exactly 64.
All inputs are finite; a program needn't handle non-finite values.
Results may differ from the reference program's by a relative error of at most 0.0057.
Values may be sent and summed in bfloat16 or wider, within the bound.
A program may use at most 64 MiB of HBM per device.

```python
import math
import jax
import jax.numpy as jnp
import numpy as np
from jax import lax

D = 5120
HEADS = 20
HD = 128
TMAX = 3
NWIN = 4
FRAMES = 8
TOK_DEV = 128
WIN = 64
TOKENS = 1024
SPATIAL = 128
BLOCKS = 8
N_HEAD = 4


def alternate(even_rows, odd_rows):
    return jnp.stack((even_rows, odd_rows), axis=1).reshape(TOKENS, HEADS * HD)


def draw_queries(key, part):
    key = jax.random.fold_in(key, 101)
    shape = (TOKENS // 2, HEADS * HD)
    even_key, odd_key = jax.random.split(key)
    even_rows = jnp.clip(jax.random.normal(even_key, shape), -4.5, 4.5)
    odd_rows = jnp.clip(jax.random.normal(odd_key, shape), -4.5, 4.5)
    return alternate(even_rows, odd_rows).astype(jnp.bfloat16)


def draw_keys(key, part):
    key = jax.random.fold_in(key, 202)
    shape = (TOKENS // 2, HEADS * HD)
    even_key, odd_key = jax.random.split(key)
    even_rows = jnp.clip(jax.random.normal(even_key, shape), -4.5, 4.5)
    odd_rows = jnp.clip(jax.random.normal(odd_key, shape), -4.5, 4.5)
    return alternate(even_rows, odd_rows).astype(jnp.bfloat16)


def draw_head_class(key, part):
    key = jax.random.fold_in(key, 303)
    count_key, full_key, order_key = jax.random.split(key, 3)
    per_group = HEADS // N_HEAD
    counts = jax.random.randint(count_key, (N_HEAD,), 1, TMAX + 1)
    full_group = jax.random.randint(full_key, (), 0, N_HEAD)
    counts = jnp.where(jnp.arange(N_HEAD, dtype=jnp.int32) == full_group, TMAX, counts)
    group_keys = jax.random.split(order_key, N_HEAD)
    orders = jax.vmap(lambda group_key: jax.random.permutation(group_key, per_group))(group_keys)
    return (orders < counts[:, None]).astype(jnp.int32).reshape(HEADS)


def block_scale(own_key, extent, cuts, smallest, largest):
    gain = 1.0
    for dim, blocks in cuts:
        draws = jax.random.uniform(jax.random.fold_in(jax.random.fold_in(own_key, 6), dim), (blocks,), jnp.float32, smallest / len(cuts), largest / len(cuts))
        gain = gain * jnp.repeat(jnp.exp(draws), extent[dim] // blocks).reshape((-1,) + (1,) * (len(extent) - 1 - dim))
    return gain


def length_profile(amount, total, reach, skew):
    weights = [(1 << 20) // math.isqrt(grade ** skew) + 1 for grade in range(2, amount + 1)]
    surplus, given = total - reach - (amount - 1), [1] * (amount - 1)
    while surplus > 0:
        candidates = [i for i in range(amount - 1) if given[i] < reach]
        pool, budget = sum([weights[i] for i in candidates]), surplus
        for i in candidates:
            extra = min(reach - given[i], max(1, budget * weights[i] // pool), surplus)
            given[i] = given[i] + extra
            surplus = surplus - extra
    return np.array([reach] + given)


def uneven_parts(rng, count, total, most, lean):
    if count == 2:
        one = jax.random.randint(rng, (), max(1, total - most), min(most, total - 1) + 1)
        return jnp.stack([one, total - one])
    tallies = jnp.asarray(length_profile(count, total, most, lean), jnp.int32)
    couples = (count - 1) // 2
    donor, sink = tallies[1:1 + 2 * couples:2], tallies[2:2 + 2 * couples:2]
    margin = jnp.minimum(donor - 1, most - sink)
    passed = jax.random.randint(jax.random.fold_in(rng, 1), (couples,), 0, 1 << 20) % (margin + 1)
    tallies = tallies.at[1:1 + 2 * couples:2].set(donor - passed).at[2:2 + 2 * couples:2].set(sink + passed)
    return tallies[jax.random.permutation(jax.random.fold_in(rng, 2), count)]


def centred(key, dims, width, bound, cuts=(), held_as=jnp.bfloat16):
    level = block_scale(key, dims, cuts, -0.22, 0.18) if cuts else 1.0
    entries = jax.random.normal(key, dims, jnp.float32) * width * level
    return jnp.minimum(jnp.maximum(entries, -bound), bound).astype(held_as)


def setup_inputs(seed: int = 0) -> dict:
    arg_keys = jax.random.split(jax.random.key(seed), 7)
    return {
        "queries": draw_queries(jax.random.fold_in(arg_keys[6], 71), 0),
        "keys": draw_keys(jax.random.fold_in(arg_keys[6], 71), 0),
        "values": centred(arg_keys[2], (TOKENS, HEADS * HD), 1.0, 6.0, ((0, 8), (1, 4))),
        "head_class": draw_head_class(jax.random.fold_in(arg_keys[6], 71), 0),
        "window_lengths": jax.vmap(lambda own: uneven_parts(own, NWIN, TOK_DEV, WIN, 0))(jax.random.split(arg_keys[4], BLOCKS)).reshape((BLOCKS, NWIN)).astype(jnp.int32),
        "out_weight": centred(arg_keys[5], (HEADS * HD, D), (HEADS * HD) ** -0.5, 0.125, ((0, 8), (1, 4))),
    }


def softmax_rows(scores):
    highest = lax.optimization_barrier(jnp.max(scores, axis=-1, keepdims=True))
    weights = jnp.exp(scores - highest)
    return weights / lax.optimization_barrier(jnp.sum(weights, axis=-1, keepdims=True))

def spatial_block(inputs):
    query, key_rows, value_rows, lengths = inputs
    scaling = 1.0 / math.sqrt(HD)
    ends = jnp.cumsum(lengths)
    positions = jnp.arange(TOK_DEV, dtype=jnp.int32)
    window_ids = lax.optimization_barrier(jnp.sum((positions[:, None] >= ends[None, :]).astype(jnp.int32), axis=1))
    same_window = window_ids[:, None] == window_ids[None, :]
    query_wide = query.reshape(TOK_DEV, HEADS, HD).astype(jnp.float32)
    key_wide = key_rows.reshape(TOK_DEV, HEADS, HD).astype(jnp.float32)
    value_wide = value_rows.reshape(TOK_DEV, HEADS, HD).astype(jnp.float32)
    scores = jnp.einsum('shd,thd->hst', query_wide, key_wide) * scaling
    scores = jnp.where(same_window[None], scores, -1e+30)
    weights = softmax_rows(scores).astype(jnp.bfloat16)
    return jnp.einsum('hst,thd->shd', weights.astype(jnp.float32), value_wide).astype(jnp.bfloat16)

def reference(queries, keys, values, head_class, window_lengths, out_weight):
    scaling = 1.0 / math.sqrt(HD)
    blocks_total = TOKENS // TOK_DEV
    cols = HEADS * HD
    spatial_out = lax.map(spatial_block, (queries.reshape(blocks_total, TOK_DEV, cols), keys.reshape(blocks_total, TOK_DEV, cols), values.reshape(blocks_total, TOK_DEV, cols), window_lengths))
    spatial_out = spatial_out.reshape(FRAMES, SPATIAL, HEADS, HD)
    block_cols = 32
    framed_q = queries.reshape(FRAMES, SPATIAL, cols)
    framed_k = keys.reshape(FRAMES, SPATIAL, cols)
    framed_v = values.reshape(FRAMES, SPATIAL, cols)

    def temporal_block(first_col):

        def pick(source):
            taken = lax.dynamic_slice_in_dim(source, first_col, block_cols, 1)
            return taken.reshape(FRAMES, block_cols, HEADS, HD).astype(jnp.float32)
        query_wide = pick(framed_q)
        key_wide = pick(framed_k)
        value_wide = pick(framed_v)
        scores = jnp.einsum('fbhd,gbhd->bhfg', query_wide, key_wide) * scaling
        weights = softmax_rows(scores).astype(jnp.bfloat16)
        return jnp.einsum('bhfg,gbhd->fbhd', weights.astype(jnp.float32), value_wide).astype(jnp.bfloat16)
    starts = (jnp.arange(SPATIAL // block_cols, dtype=jnp.int32) * block_cols).astype(jnp.int32)
    blocks = lax.map(temporal_block, starts)
    temporal_out = jnp.transpose(blocks, (1, 0, 2, 3, 4)).reshape(FRAMES, SPATIAL, HEADS, HD)
    chosen = (head_class == 1)[None, None, :, None]
    mixed = jnp.where(chosen, temporal_out, spatial_out)
    flat = mixed.reshape(TOKENS, cols)
    return jnp.dot(flat, out_weight, preferred_element_type=jnp.float32).astype(jnp.bfloat16)
```

```python
import functools
import math

import jax
import jax.numpy as jnp
from jax import lax
from jax.experimental import pallas as pl
from jax.experimental.pallas import tpu as pltpu
from jax.sharding import PartitionSpec as P

HD = 128
TMAX = 3
FRAMES = 8


def softmax_rows(scores):
    highest = jnp.max(scores, axis=-1, keepdims=True)
    weights = jnp.exp(scores - highest)
    return weights / jnp.sum(weights, axis=-1, keepdims=True)


def compact_heads(source, picker):
    return jnp.einsum("shd,th->std", source, picker, preferred_element_type=jnp.float32).astype(
        jnp.bfloat16
    )


def expand_heads(source, picker):
    return jnp.einsum("std,th->shd", source, picker, preferred_element_type=jnp.float32).astype(
        jnp.bfloat16
    )


def window_attention(query, key_rows, value_rows, lengths, scaling):
    ends = jnp.cumsum(lengths)
    positions = jnp.arange(query.shape[0], dtype=jnp.int32)
    window_ids = jnp.sum((positions[:, None] >= ends[None, :]).astype(jnp.int32), axis=1)
    same_window = window_ids[:, None] == window_ids[None, :]
    scores = (
        jnp.einsum("shd,thd->hst", query, key_rows, preferred_element_type=jnp.float32) * scaling
    )
    scores = jnp.where(same_window[None], scores, -1e30)
    weights = softmax_rows(scores).astype(jnp.bfloat16)
    return jnp.einsum(
        "hst,thd->shd", weights, value_rows, preferred_element_type=jnp.float32
    ).astype(jnp.bfloat16)


def gather_body(queries, keys, values, head_class, window_lengths, out_weight):
    tok_len, columns = queries.shape
    local_heads = columns // HD
    scaling = 1.0 / math.sqrt(HD)
    head_group = lax.axis_index("head")
    classes = lax.dynamic_slice_in_dim(head_class, head_group * local_heads, local_heads)
    temporal_mask = classes == 1
    slot_rank = jnp.cumsum(temporal_mask.astype(jnp.int32)) - 1
    slot_ids = jnp.arange(TMAX, dtype=jnp.int32)
    picker = ((slot_rank[None, :] == slot_ids[:, None]) & temporal_mask[None, :]).astype(
        jnp.bfloat16
    )
    shaped = [array_in.reshape(tok_len, local_heads, HD) for array_in in (queries, keys, values)]
    lengths = window_lengths[0]
    spatial_out = window_attention(shaped[0], shaped[1], shaped[2], lengths, scaling)
    packed = [compact_heads(array_in, picker)[None] for array_in in shaped]
    query = lax.all_to_all(packed[0], "seq", split_axis=1, concat_axis=0, tiled=True)
    key_rows = lax.all_to_all(packed[1], "seq", split_axis=1, concat_axis=0, tiled=True)
    value_rows = lax.all_to_all(packed[2], "seq", split_axis=1, concat_axis=0, tiled=True)
    sources, width, count, size = query.shape
    groups = sources // FRAMES
    query = query.reshape(FRAMES, groups, width, count, size)
    key_rows = key_rows.reshape(FRAMES, groups, width, count, size)
    value_rows = value_rows.reshape(FRAMES, groups, width, count, size)
    scores = (
        jnp.einsum("fjcnd,gjcnd->jcnfg", query, key_rows, preferred_element_type=jnp.float32)
        * scaling
    )
    weights = softmax_rows(scores).astype(jnp.bfloat16)
    attended = jnp.einsum(
        "jcnfg,gjcnd->fjcnd", weights, value_rows, preferred_element_type=jnp.float32
    ).astype(jnp.bfloat16)
    attended = attended.reshape(sources, width, count, size)
    returned = lax.all_to_all(attended, "seq", split_axis=0, concat_axis=1, tiled=True)
    temporal_out = expand_heads(returned[0], picker)
    mixed = jnp.where(temporal_mask[None, :, None], temporal_out, spatial_out)
    mixed_local = mixed.reshape(tok_len, local_heads * HD)
    mixed_all = lax.all_gather(mixed_local, "head", axis=1, tiled=True)
    summed = jnp.dot(
        mixed_all,
        lax.all_gather(out_weight, "seq", axis=0, tiled=True),
        preferred_element_type=jnp.float32,
    )
    return summed.astype(jnp.bfloat16)


MESH = pl.DeviceIdType.MESH
CHUNKS = 2


def masked_attention(query, key_rows, value_rows, same, scaling):
    scores = lax.dot_general(
        query, key_rows, (((1,), (1,)), ((), ())), preferred_element_type=jnp.float32
    )
    scores = jnp.where(same, scores * scaling, -1e30)
    weights = softmax_rows(scores).astype(jnp.bfloat16)
    return jnp.dot(weights, value_rows, preferred_element_type=jnp.float32).astype(jnp.bfloat16)


def slot_conditions(class_ref, first, local_heads):
    rank = jnp.int32(0)
    taken = []
    for h in range(local_heads):
        flag = (class_ref[first + h] == 1).astype(jnp.int32)
        taken.append([flag * (rank == t).astype(jnp.int32) == 1 for t in range(TMAX)])
        rank = rank + flag
    return taken


def layer_kernel(
    n, groups, class_ref, len_ref, q_ref, k_ref, v_ref, w_ref, out_ref,
    packed, landed, spat, spat_in, tsend, temp_in, mixed, w_all,
    up_in, up_out, down_in, down_out,
    qkv_s, qkv_r, w_s, w_r, w_l, sp_s, sp_r, sp_l, spf_s, t_s, t_r, t_l, tf_s,
    up_s, up_r, down_s, down_r,
):
    pair = n // groups
    seq, head = lax.axis_index("seq"), lax.axis_index("head")
    plane, lane = seq // pair, lax.rem(seq, pair)
    core = lax.rem(head, 2)
    sibling = head + 1 - 2 * core
    tok, columns = q_ref.shape
    local_heads = columns // HD
    width = tok // n
    rows = w_ref.shape[0]
    scaling = 1.0 / math.sqrt(HD)

    def send(src, dst, send_sem, recv_sem, to_seq, to_head):
        return pltpu.make_async_remote_copy(
            src_ref=src, dst_ref=dst, send_sem=send_sem, recv_sem=recv_sem,
            device_id=(to_seq, to_head), device_id_type=MESH,
        )

    own_w = pltpu.make_async_copy(w_ref, w_all.at[lane], w_l)
    own_w.start()

    barrier = pltpu.get_barrier_semaphore()

    def greet(to_seq, to_head):
        pl.semaphore_signal(barrier, inc=1, device_id=(to_seq, to_head), device_id_type=MESH)

    for step in range(1, n):
        greet(lax.rem(seq + step, n), head)
    greet(seq, sibling)

    @pl.when(plane != head)
    def _():
        for peer in range(n):
            greet(jnp.int32(peer), plane)

    taken = slot_conditions(class_ref, head * local_heads, local_heads)
    for a, ref in enumerate((q_ref, k_ref, v_ref)):
        for t in range(TMAX):
            value = jnp.zeros((tok, HD), jnp.bfloat16)
            for h in range(t, local_heads):
                value = jnp.where(taken[h][t], ref[:, h * HD:(h + 1) * HD], value)
            at = (a * TMAX + t) * HD
            packed[:, :, at:at + HD] = value.reshape(n, width, HD)

    @pl.when(plane == 0)
    def _():
        up_in[...] = jnp.zeros_like(up_in)

    @pl.when(plane == groups - 1)
    def _():
        down_in[...] = jnp.zeros_like(down_in)

    pl.semaphore_wait(barrier, (n - 1) + pair * (groups - 1) + 1)

    qkv = []
    for step in range(1, n):
        peer = lax.rem(seq + step, n)
        copy = send(packed.at[peer], landed.at[seq], qkv_s.at[peer], qkv_r.at[seq], peer, head)
        copy.start()
        qkv.append(copy)
    landed[seq] = packed[seq]

    other = plane * pair + (1 - lane)
    w_copy = send(w_ref, w_all.at[lane], w_s, w_r.at[lane], other, head)
    w_copy.start()

    def window_of(axis):
        position = lax.broadcasted_iota(jnp.int32, (tok, tok), axis)
        ids = jnp.zeros((tok, tok), jnp.int32)
        end = jnp.int32(0)
        for i in range(len_ref.shape[1]):
            end = end + len_ref[0, i]
            ids = ids + (position >= end).astype(jnp.int32)
        return ids

    same_window = window_of(0) == window_of(1)
    for h in range(local_heads):
        at = slice(h * HD, (h + 1) * HD)
        spat[:, at] = masked_attention(q_ref[:, at], k_ref[:, at], v_ref[:, at], same_window, scaling)

    sp_core = lax.rem(plane, 2)
    sp_copies = []
    for y in range(groups // 2):
        to_seq, to_head = head * pair + lane, 2 * y + sp_core
        mine = (to_seq == seq) & (to_head == head)
        copy = send(spat, spat_in.at[plane], sp_s.at[y], sp_r.at[plane], to_seq, to_head)
        sp_copies.append((mine, copy))

        @pl.when(jnp.logical_not(mine))
        def _(copy=copy):
            copy.start()

        @pl.when(mine)
        def _():
            spat_in[plane] = spat[...]

    for step in range(1, n):
        peer = lax.rem(seq + n - step, n)
        send(landed.at[peer], landed.at[peer], qkv_s.at[peer], qkv_r.at[peer], peer, head).wait_recv()
    row = lax.rem(lax.broadcasted_iota(jnp.int32, (tok, tok), 0), width)
    column = lax.rem(lax.broadcasted_iota(jnp.int32, (tok, tok), 1), width)
    same_position = row == column
    for t in range(TMAX):
        query, key_rows, value_rows = (
            landed[:, :, (a * TMAX + t) * HD:(a * TMAX + t + 1) * HD].reshape(tok, HD)
            for a in range(3)
        )
        result = masked_attention(query, key_rows, value_rows, same_position, scaling)
        for f in range(n):
            tsend[f % pair, f // pair, :, t * HD:(t + 1) * HD] = result[f * width:(f + 1) * width]

    t_core = lax.rem(seq, 2)
    t_copies = []
    for x in range(pair):
        for y in range(groups // 2):
            to_seq, to_head = head * pair + x, 2 * y + t_core
            mine = (to_seq == seq) & (to_head == head)
            copy = send(tsend.at[x], temp_in.at[seq], t_s.at[x, y], t_r.at[seq], to_seq, to_head)
            t_copies.append((mine, copy))

            @pl.when(jnp.logical_not(mine))
            def _(copy=copy):
                copy.start()

            @pl.when(mine)
            def _(x=x):
                temp_in[seq] = tsend[x]

    forwards = []
    for j in range(groups // 2):
        source = 2 * j + core
        here = (source == plane) & (plane == head)
        copy = send(spat_in.at[source], spat_in.at[source], spf_s.at[j], sp_r.at[source], seq, sibling)

        @pl.when(jnp.logical_not(here))
        def _(copy=copy):
            copy.wait_recv()

        copy.start()
        forwards.append(copy)
    for j in range(n // 2):
        source = 2 * j + core
        here = (source == seq) & (plane == head)
        copy = send(temp_in.at[source], temp_in.at[source], tf_s.at[j], t_r.at[source], seq, sibling)

        @pl.when(jnp.logical_not(here))
        def _(copy=copy):
            copy.wait_recv()

        copy.start()
        forwards.append(copy)
    for j in range(groups // 2):
        source = 2 * j + 1 - core
        send(spat_in.at[source], spat_in.at[source], spf_s.at[j], sp_r.at[source], seq, sibling).wait_recv()
    for j in range(n // 2):
        source = 2 * j + 1 - core
        send(temp_in.at[source], temp_in.at[source], tf_s.at[j], t_r.at[source], seq, sibling).wait_recv()

    taken = slot_conditions(class_ref, plane * local_heads, local_heads)
    for z in range(groups):
        for h in range(local_heads):
            value = spat_in[z, :, h * HD:(h + 1) * HD]
            for t in range(min(h + 1, TMAX)):
                slot = temp_in[:, z, :, t * HD:(t + 1) * HD].reshape(tok, HD)
                value = jnp.where(taken[h][t], slot, value)
            mixed[z, :, h * HD:(h + 1) * HD] = value

    own_w.wait()
    send(w_ref, w_all.at[1 - lane], w_s, w_r.at[1 - lane], other, head).wait_recv()

    chunk = w_ref.shape[1] // CHUNKS

    def product(z, c):
        weight = w_all[:, :, c * chunk:(c + 1) * chunk].reshape(pair * rows, chunk)
        return jnp.dot(mixed[z], weight, preferred_element_type=jnp.float32)

    ways = ((1, up_in, up_out, up_s, up_r), (-1, down_in, down_out, down_s, down_r))

    def onward(way, d, c):
        sign, came, goes, s_sem, r_sem = way
        to_seq = seq + sign * pair
        return send(goes.at[d - 1, c], came.at[d - 1, c], s_sem.at[d - 1, c], r_sem.at[d - 1, c], to_seq, head)

    def has_previous(way):
        return plane > 0 if way[0] == 1 else plane < groups - 1

    def reaches(way, d):
        return plane + d < groups if way[0] == 1 else plane >= d

    def arrive(way, d, c):
        @pl.when(has_previous(way))
        def _():
            sign, came, goes, s_sem, r_sem = way
            send(goes.at[d, c], came.at[d, c], s_sem.at[d, c], r_sem.at[d, c], seq, head).wait_recv()

    for d in range(groups - 1, 0, -1):
        for c in range(CHUNKS):
            for way in ways:
                @pl.when(reaches(way, d))
                def _(way=way, d=d, c=c):
                    total = product(plane + way[0] * d, c)
                    if d < groups - 1:
                        arrive(way, d, c)
                        total = total + way[1][d, c].astype(jnp.float32)
                    way[2][d - 1, c] = total.astype(jnp.bfloat16)
                    onward(way, d, c).start()
    for c in range(CHUNKS):
        total = product(plane, c)
        for way in ways:
            arrive(way, 0, c)
            total = total + way[1][0, c].astype(jnp.float32)
        out_ref[:, c * chunk:(c + 1) * chunk] = total.astype(jnp.bfloat16)

    for copy in qkv:
        copy.wait_send()
    w_copy.wait_send()
    for mine, copy in sp_copies + t_copies:
        @pl.when(jnp.logical_not(mine))
        def _(copy=copy):
            copy.wait_send()
    for copy in forwards:
        copy.wait_send()
    for d in range(groups - 1, 0, -1):
        for c in range(CHUNKS):
            for way in ways:
                @pl.when(reaches(way, d))
                def _(way=way, d=d, c=c):
                    onward(way, d, c).wait_send()


def kernel_body(n, groups, queries, keys, values, head_class, window_lengths, out_weight):
    tok, columns = queries.shape
    rows, out_columns = out_weight.shape
    pair, width = n // groups, tok // n
    chunk = out_columns // CHUNKS
    bf16, dma = jnp.bfloat16, pltpu.SemaphoreType.DMA
    vmem = pl.BlockSpec(memory_space=pltpu.VMEM)
    smem = pl.BlockSpec(memory_space=pltpu.SMEM)
    line = (groups - 1, CHUNKS)
    return pl.pallas_call(
        functools.partial(layer_kernel, n, groups),
        out_shape=jax.ShapeDtypeStruct((tok, out_columns), bf16),
        in_specs=[smem, smem, vmem, vmem, vmem, pl.BlockSpec(memory_space=pl.ANY)],
        out_specs=vmem,
        scratch_shapes=[
            pltpu.VMEM((n, width, 3 * TMAX * HD), bf16),
            pltpu.VMEM((n, width, 3 * TMAX * HD), bf16),
            pltpu.VMEM((tok, columns), bf16),
            pltpu.VMEM((groups, tok, columns), bf16),
            pltpu.VMEM((pair, groups, width, TMAX * HD), bf16),
            pltpu.VMEM((n, groups, width, TMAX * HD), bf16),
            pltpu.VMEM((groups, tok, columns), bf16),
            pltpu.VMEM((pair, rows, out_columns), bf16),
            pltpu.VMEM(line + (tok, chunk), bf16),
            pltpu.VMEM(line + (tok, chunk), bf16),
            pltpu.VMEM(line + (tok, chunk), bf16),
            pltpu.VMEM(line + (tok, chunk), bf16),
            dma((n,)), dma((n,)),
            dma, dma((pair,)), dma,
            dma((groups // 2,)), dma((groups,)), dma, dma((groups // 2,)),
            dma((pair, groups // 2)), dma((n,)), dma, dma((n // 2,)),
            dma(line), dma(line), dma(line), dma(line),
        ],
        compiler_params=pltpu.CompilerParams(
            collective_id=0, has_side_effects=True, vmem_limit_bytes=32 * 1024 * 1024
        ),
        cost_estimate=pl.CostEstimate(
            flops=2 * groups * tok * columns * out_columns,
            bytes_accessed=4 * rows * out_columns,
            transcendentals=local_count(columns) * tok * tok,
        ),
    )(head_class, window_lengths, queries, keys, values, out_weight)


def local_count(columns):
    return columns // HD + TMAX


def solution(mesh):
    n, groups = mesh.shape["seq"], mesh.shape["head"]

    def body(queries, keys, values, head_class, window_lengths, out_weight):
        tok, rows = queries.shape[0], out_weight.shape[0]
        if n == FRAMES and n == 2 * groups and rows > tok:
            return kernel_body(
                n, groups, queries, keys, values, head_class, window_lengths, out_weight
            )
        return gather_body(queries, keys, values, head_class, window_lengths, out_weight)

    placed = (
        P("seq", "head"),
        P("seq", "head"),
        P("seq", "head"),
        P(),
        P("seq", None),
        P("seq", "head"),
    )
    return jax.shard_map(
        body, mesh=mesh, in_specs=placed, out_specs=P("seq", "head"), check_vma=False
    )
```

```python
import functools
import math

import jax
import jax.numpy as jnp
from jax import lax
from jax.experimental import pallas as pl
from jax.experimental.pallas import tpu as pltpu
from jax.sharding import PartitionSpec as P

HD = 128
TMAX = 3
FRAMES = 8


def softmax_rows(scores):
    highest = jnp.max(scores, axis=-1, keepdims=True)
    weights = jnp.exp(scores - highest)
    return weights / jnp.sum(weights, axis=-1, keepdims=True)


def compact_heads(source, picker):
    return jnp.einsum("shd,th->std", source, picker, preferred_element_type=jnp.float32).astype(
        jnp.bfloat16
    )


def expand_heads(source, picker):
    return jnp.einsum("std,th->shd", source, picker, preferred_element_type=jnp.float32).astype(
        jnp.bfloat16
    )


def window_attention(query, key_rows, value_rows, lengths, scaling):
    ends = jnp.cumsum(lengths)
    positions = jnp.arange(query.shape[0], dtype=jnp.int32)
    window_ids = jnp.sum((positions[:, None] >= ends[None, :]).astype(jnp.int32), axis=1)
    same_window = window_ids[:, None] == window_ids[None, :]
    scores = (
        jnp.einsum("shd,thd->hst", query, key_rows, preferred_element_type=jnp.float32) * scaling
    )
    scores = jnp.where(same_window[None], scores, -1e30)
    weights = softmax_rows(scores).astype(jnp.bfloat16)
    return jnp.einsum(
        "hst,thd->shd", weights, value_rows, preferred_element_type=jnp.float32
    ).astype(jnp.bfloat16)


def gather_body(queries, keys, values, head_class, window_lengths, out_weight):
    tok_len, columns = queries.shape
    local_heads = columns // HD
    scaling = 1.0 / math.sqrt(HD)
    head_group = lax.axis_index("head")
    classes = lax.dynamic_slice_in_dim(head_class, head_group * local_heads, local_heads)
    temporal_mask = classes == 1
    slot_rank = jnp.cumsum(temporal_mask.astype(jnp.int32)) - 1
    slot_ids = jnp.arange(TMAX, dtype=jnp.int32)
    picker = ((slot_rank[None, :] == slot_ids[:, None]) & temporal_mask[None, :]).astype(
        jnp.bfloat16
    )
    shaped = [array_in.reshape(tok_len, local_heads, HD) for array_in in (queries, keys, values)]
    lengths = window_lengths[0]
    spatial_out = window_attention(shaped[0], shaped[1], shaped[2], lengths, scaling)
    packed = [compact_heads(array_in, picker)[None] for array_in in shaped]
    query = lax.all_to_all(packed[0], "seq", split_axis=1, concat_axis=0, tiled=True)
    key_rows = lax.all_to_all(packed[1], "seq", split_axis=1, concat_axis=0, tiled=True)
    value_rows = lax.all_to_all(packed[2], "seq", split_axis=1, concat_axis=0, tiled=True)
    sources, width, count, size = query.shape
    groups = sources // FRAMES
    query = query.reshape(FRAMES, groups, width, count, size)
    key_rows = key_rows.reshape(FRAMES, groups, width, count, size)
    value_rows = value_rows.reshape(FRAMES, groups, width, count, size)
    scores = (
        jnp.einsum("fjcnd,gjcnd->jcnfg", query, key_rows, preferred_element_type=jnp.float32)
        * scaling
    )
    weights = softmax_rows(scores).astype(jnp.bfloat16)
    attended = jnp.einsum(
        "jcnfg,gjcnd->fjcnd", weights, value_rows, preferred_element_type=jnp.float32
    ).astype(jnp.bfloat16)
    attended = attended.reshape(sources, width, count, size)
    returned = lax.all_to_all(attended, "seq", split_axis=0, concat_axis=1, tiled=True)
    temporal_out = expand_heads(returned[0], picker)
    mixed = jnp.where(temporal_mask[None, :, None], temporal_out, spatial_out)
    mixed_local = mixed.reshape(tok_len, local_heads * HD)
    mixed_all = lax.all_gather(mixed_local, "head", axis=1, tiled=True)
    summed = jnp.dot(
        mixed_all,
        lax.all_gather(out_weight, "seq", axis=0, tiled=True),
        preferred_element_type=jnp.float32,
    )
    return summed.astype(jnp.bfloat16)


MESH = pl.DeviceIdType.MESH
CHUNKS = 5
EARLY = 3
VMEM_LIMIT = 62 * 1024 * 1024


def masked_attention(query, key_rows, value_rows, same, scaling):
    scores = lax.dot_general(
        query, key_rows, (((1,), (1,)), ((), ())), preferred_element_type=jnp.float32
    )
    scores = jnp.where(same, scores * scaling, -1e30)
    weights = softmax_rows(scores).astype(jnp.bfloat16)
    return jnp.dot(weights, value_rows, preferred_element_type=jnp.float32).astype(jnp.bfloat16)


def slot_conditions(class_ref, first, local_heads):
    rank = jnp.int32(0)
    taken = []
    for h in range(local_heads):
        flag = (class_ref[first + h] == 1).astype(jnp.int32)
        taken.append([flag * (rank == t).astype(jnp.int32) == 1 for t in range(TMAX)])
        rank = rank + flag
    return taken


def layer_kernel(
    n, groups, class_hbm, len_hbm, q_hbm, k_hbm, v_hbm, w_ref, out_ref,
    class_ref, len_ref, q_ref, k_ref, v_ref,
    packed, landed, spat, spat_in, tsend, temp_in, mixed, w_all,
    up_in, up_out, down_in, down_out,
    load_s, qkv_s, qkv_r, w_s, w_r, w_l, sp_s, sp_r, share_s, share_r, t_s, t_r,
    up_s, up_r, down_s, down_r,
):
    pair = n // groups
    seq, head = lax.axis_index("seq"), lax.axis_index("head")
    plane, lane = seq // pair, lax.rem(seq, pair)
    rank = lane * groups + head
    core = lax.rem(head, 2)
    sibling = head + 1 - 2 * core
    across = lax.rem(head + groups // 2, groups)
    at_home = plane == head
    tok, columns = q_ref.shape
    local_heads = columns // HD
    width, quarter = tok // n, tok // groups
    rows = w_ref.shape[0]
    chunk = w_ref.shape[1] // CHUNKS
    scaling = 1.0 / math.sqrt(HD)

    def send(src, dst, send_sem, recv_sem, to_seq, to_head):
        return pltpu.make_async_remote_copy(
            src_ref=src, dst_ref=dst, send_sem=send_sem, recv_sem=recv_sem,
            device_id=(to_seq, to_head), device_id_type=MESH,
        )

    loads = [
        pltpu.make_async_copy(src, dst, load_s.at[i])
        for i, (src, dst) in enumerate(
            ((class_hbm, class_ref), (q_hbm, q_ref), (k_hbm, k_ref), (v_hbm, v_ref), (len_hbm, len_ref))
        )
    ]
    for load in loads:
        load.start()
    own_w = pltpu.make_async_copy(w_ref, w_all.at[lane], w_l)
    own_w.start()

    barrier = pltpu.get_barrier_semaphore()

    def greet(to_seq, to_head):
        pl.semaphore_signal(barrier, inc=1, device_id=(to_seq, to_head), device_id_type=MESH)

    for step in range(1, n):
        other = lax.rem(rank + step, n)
        greet(plane * pair + other // groups, lax.rem(other, groups))
    for step in range(1, groups):
        for x in range(pair):
            greet(lax.rem(plane + step, groups) * pair + x, plane)

    @pl.when(plane > 0)
    def _():
        greet(seq - pair, head)

    @pl.when(plane < groups - 1)
    def _():
        greet(seq + pair, head)

    for load in loads[:4]:
        load.wait()

    taken = slot_conditions(class_ref, head * local_heads, local_heads)
    for a, ref in enumerate((q_ref, k_ref, v_ref)):
        for t in range(TMAX):
            value = jnp.zeros((tok, HD), jnp.bfloat16)
            for h in range(t, local_heads):
                value = jnp.where(taken[h][t], ref[:, h * HD:(h + 1) * HD], value)
            at = (a * TMAX + t) * HD
            packed[:, :, at:at + HD] = value.reshape(n, width, HD)

    @pl.when(plane == 0)
    def _():
        up_in[...] = jnp.zeros_like(up_in)

    @pl.when(plane == groups - 1)
    def _():
        down_in[...] = jnp.zeros_like(down_in)

    greeted = n - 1 + (plane > 0).astype(jnp.int32) + (plane < groups - 1).astype(jnp.int32)
    pl.semaphore_wait(barrier, greeted + n * jnp.logical_not(at_home).astype(jnp.int32))

    def qkv_copy(step):
        to = lax.rem(rank + step, n)
        return send(
            packed.at[to], landed.at[seq], qkv_s.at[to], qkv_r.at[seq],
            head * pair + to // groups, lax.rem(to, groups),
        )

    for step in range(1, n):
        qkv_copy(step).start()

    @pl.when(jnp.logical_not(at_home))
    def _():
        qkv_copy(0).start()

    @pl.when(at_home)
    def _():
        landed[seq] = packed[rank]

    def w_copy(c, owner):
        cols = pl.ds(c * chunk, chunk)
        return send(
            w_ref.at[:, cols], w_all.at[owner, :, cols], w_s.at[c], w_r.at[c],
            plane * pair + (1 - lane), head,
        )

    for c in range(EARLY):
        w_copy(c, lane).start()

    loads[4].wait()

    def window_of(axis):
        position = lax.broadcasted_iota(jnp.int32, (tok, tok), axis)
        ids = jnp.zeros((tok, tok), jnp.int32)
        end = jnp.int32(0)
        for i in range(len_ref.shape[1]):
            end = end + len_ref[0, i]
            ids = ids + (position >= end).astype(jnp.int32)
        return ids

    same_window = window_of(0) == window_of(1)
    for h in range(local_heads):
        at = slice(h * HD, (h + 1) * HD)
        value = masked_attention(q_ref[:, at], k_ref[:, at], v_ref[:, at], same_window, scaling)
        spat[:, :, at] = value.reshape(groups, quarter, HD)

    def spatial_copy(step):
        to = lax.rem(head + step, groups)
        return send(
            spat.at[to], spat_in.at[to, plane], sp_s.at[to], sp_r.at[plane], head * pair + lane, to
        )

    for step in range(1, groups):
        spatial_copy(step).start()

    @pl.when(jnp.logical_not(at_home))
    def _():
        spatial_copy(0).start()

    @pl.when(at_home)
    def _():
        spat_in[head, plane] = spat[head]

    for source in range(n):
        @pl.when(jnp.logical_not(at_home & (seq == source)))
        def _(source=source):
            send(
                landed.at[source], landed.at[source], qkv_s.at[source], qkv_r.at[source], seq, head
            ).wait_recv()

    for z in range(groups):
        @pl.when(jnp.logical_not(at_home & (plane == z)))
        def _(z=z):
            send(
                spat.at[z], spat_in.at[head, z], sp_s.at[z], sp_r.at[z], seq, head
            ).wait_recv()

    def share(which, slot, to_head):
        return send(spat_in.at[which], spat_in.at[which], share_s.at[slot], share_r.at[which], seq, to_head)

    share(head, 0, across).start()
    share(head, 1, sibling).start()

    row = lax.rem(lax.broadcasted_iota(jnp.int32, (tok, tok), 0), width)
    column = lax.rem(lax.broadcasted_iota(jnp.int32, (tok, tok), 1), width)
    same_position = row == column
    for t in range(TMAX):
        query, key_rows, value_rows = (
            landed[:, :, (a * TMAX + t) * HD:(a * TMAX + t + 1) * HD].reshape(tok, HD)
            for a in range(3)
        )
        result = masked_attention(query, key_rows, value_rows, same_position, scaling)
        for f in range(n):
            tsend[f % pair, f // pair, :, t * HD:(t + 1) * HD] = result[f * width:(f + 1) * width]

    def temporal_copy(step):
        to = lax.rem(rank + step, n)
        x = to // groups
        return send(
            tsend.at[x], temp_in.at[rank], t_s.at[to], t_r.at[rank], plane * pair + x, lax.rem(to, groups)
        )

    for step in range(1, n):
        temporal_copy(step).start()
    temp_in[rank] = tsend[lane]
    for c in range(EARLY, CHUNKS):
        w_copy(c, lane).start()

    share(across, 0, across).wait_recv()
    share(across, 2, sibling).start()
    share(sibling, 1, sibling).wait_recv()
    share(lax.rem(sibling + groups // 2, groups), 2, sibling).wait_recv()
    for step in range(1, n):
        source = lax.rem(rank + n - step, n)
        send(
            temp_in.at[source], temp_in.at[source], t_s.at[source], t_r.at[source], seq, head
        ).wait_recv()

    taken = slot_conditions(class_ref, plane * local_heads, local_heads)
    for z in range(groups):
        for h in range(local_heads):
            value = spat_in[:, z, :, h * HD:(h + 1) * HD].reshape(tok, HD)
            for t in range(min(h + 1, TMAX)):
                slot = temp_in[:, z, :, t * HD:(t + 1) * HD].reshape(tok, HD)
                value = jnp.where(taken[h][t], slot, value)
            mixed[z, :, h * HD:(h + 1) * HD] = value

    own_w.wait()

    def product(z, c):
        weight = w_all[:, :, c * chunk:(c + 1) * chunk].reshape(pair * rows, chunk)
        return jnp.dot(mixed[z], weight, preferred_element_type=jnp.float32)

    ways = ((1, up_in, up_out, up_s, up_r), (-1, down_in, down_out, down_s, down_r))

    def onward(way, d, c):
        sign, came, goes, s_sem, r_sem = way
        to_seq = seq + sign * pair
        return send(goes.at[d - 1, c], came.at[d - 1, c], s_sem.at[d - 1, c], r_sem.at[d - 1, c], to_seq, head)

    def has_previous(way):
        return plane > 0 if way[0] == 1 else plane < groups - 1

    def reaches(way, d):
        return plane + d < groups if way[0] == 1 else plane >= d

    def arrive(way, d, c):
        @pl.when(has_previous(way))
        def _():
            sign, came, goes, s_sem, r_sem = way
            send(goes.at[d, c], came.at[d, c], s_sem.at[d, c], r_sem.at[d, c], seq, head).wait_recv()

    for c in range(CHUNKS):
        w_copy(c, 1 - lane).wait_recv()
        for d in range(groups - 1, 0, -1):
            for way in ways:
                @pl.when(reaches(way, d))
                def _(way=way, d=d, c=c):
                    total = product(plane + way[0] * d, c)
                    if d < groups - 1:
                        arrive(way, d, c)
                        total = total + way[1][d, c].astype(jnp.float32)
                    way[2][d - 1, c] = total.astype(jnp.bfloat16)
                    onward(way, d, c).start()
    for c in range(CHUNKS):
        total = product(plane, c)
        for way in ways:
            arrive(way, 0, c)
            total = total + way[1][0, c].astype(jnp.float32)
        out_ref[:, c * chunk:(c + 1) * chunk] = total.astype(jnp.bfloat16)

    @pl.when(jnp.logical_not(at_home))
    def _():
        qkv_copy(0).wait_send()
        spatial_copy(0).wait_send()

    for step in range(1, n):
        qkv_copy(step).wait_send()
        temporal_copy(step).wait_send()
    for step in range(1, groups):
        spatial_copy(step).wait_send()
    share(head, 0, across).wait_send()
    share(head, 1, sibling).wait_send()
    share(across, 2, sibling).wait_send()
    for c in range(CHUNKS):
        w_copy(c, lane).wait_send()
    for d in range(groups - 1, 0, -1):
        for c in range(CHUNKS):
            for way in ways:
                @pl.when(reaches(way, d))
                def _(way=way, d=d, c=c):
                    onward(way, d, c).wait_send()


def kernel_body(n, groups, queries, keys, values, head_class, window_lengths, out_weight):
    tok, columns = queries.shape
    rows, out_columns = out_weight.shape
    pair, width, quarter = n // groups, tok // n, tok // groups
    chunk = out_columns // CHUNKS
    bf16, dma = jnp.bfloat16, pltpu.SemaphoreType.DMA
    line = (groups - 1, CHUNKS)
    return pl.pallas_call(
        functools.partial(layer_kernel, n, groups),
        out_shape=jax.ShapeDtypeStruct((tok, out_columns), bf16),
        in_specs=[pl.BlockSpec(memory_space=pl.ANY)] * 6,
        out_specs=pl.BlockSpec(memory_space=pltpu.VMEM),
        scratch_shapes=[
            pltpu.SMEM(head_class.shape, jnp.int32),
            pltpu.SMEM(window_lengths.shape, jnp.int32),
            pltpu.VMEM((tok, columns), bf16),
            pltpu.VMEM((tok, columns), bf16),
            pltpu.VMEM((tok, columns), bf16),
            pltpu.VMEM((n, width, 3 * TMAX * HD), bf16),
            pltpu.VMEM((n, width, 3 * TMAX * HD), bf16),
            pltpu.VMEM((groups, quarter, columns), bf16),
            pltpu.VMEM((groups, groups, quarter, columns), bf16),
            pltpu.VMEM((pair, groups, width, TMAX * HD), bf16),
            pltpu.VMEM((n, groups, width, TMAX * HD), bf16),
            pltpu.VMEM((groups, tok, columns), bf16),
            pltpu.VMEM((pair, rows, out_columns), bf16),
            pltpu.VMEM(line + (tok, chunk), bf16),
            pltpu.VMEM(line + (tok, chunk), bf16),
            pltpu.VMEM(line + (tok, chunk), bf16),
            pltpu.VMEM(line + (tok, chunk), bf16),
            dma((5,)), dma((n,)), dma((n,)),
            dma((CHUNKS,)), dma((CHUNKS,)), dma,
            dma((groups,)), dma((groups,)), dma((3,)), dma((groups,)),
            dma((n,)), dma((n,)),
            dma(line), dma(line), dma(line), dma(line),
        ],
        compiler_params=pltpu.CompilerParams(
            collective_id=0, has_side_effects=True, vmem_limit_bytes=VMEM_LIMIT
        ),
        cost_estimate=pl.CostEstimate(
            flops=2 * groups * tok * columns * out_columns,
            bytes_accessed=4 * rows * out_columns,
            transcendentals=local_count(columns) * tok * tok,
        ),
    )(head_class, window_lengths, queries, keys, values, out_weight)


def local_count(columns):
    return columns // HD + TMAX


def solution(mesh):
    n, groups = mesh.shape["seq"], mesh.shape["head"]

    def body(queries, keys, values, head_class, window_lengths, out_weight):
        tok, rows = queries.shape[0], out_weight.shape[0]
        if n == FRAMES and n == 2 * groups and rows > tok:
            return kernel_body(
                n, groups, queries, keys, values, head_class, window_lengths, out_weight
            )
        return gather_body(queries, keys, values, head_class, window_lengths, out_weight)

    placed = (
        P("seq", "head"),
        P("seq", "head"),
        P("seq", "head"),
        P(),
        P("seq", None),
        P("seq", "head"),
    )
    return jax.shard_map(
        body, mesh=mesh, in_specs=placed, out_specs=P("seq", "head"), check_vma=False
    )
```

```python
import functools
import math

import jax
import jax.numpy as jnp
from jax import lax
from jax.experimental import pallas as pl
from jax.experimental.pallas import tpu as pltpu
from jax.sharding import PartitionSpec as P

HD = 128
TMAX = 3
FRAMES = 8


def softmax_rows(scores):
    highest = jnp.max(scores, axis=-1, keepdims=True)
    weights = jnp.exp(scores - highest)
    return weights / jnp.sum(weights, axis=-1, keepdims=True)


def compact_heads(source, picker):
    return jnp.einsum("shd,th->std", source, picker, preferred_element_type=jnp.float32).astype(
        jnp.bfloat16
    )


def expand_heads(source, picker):
    return jnp.einsum("std,th->shd", source, picker, preferred_element_type=jnp.float32).astype(
        jnp.bfloat16
    )


def window_attention(query, key_rows, value_rows, lengths, scaling):
    ends = jnp.cumsum(lengths)
    positions = jnp.arange(query.shape[0], dtype=jnp.int32)
    window_ids = jnp.sum((positions[:, None] >= ends[None, :]).astype(jnp.int32), axis=1)
    same_window = window_ids[:, None] == window_ids[None, :]
    scores = (
        jnp.einsum("shd,thd->hst", query, key_rows, preferred_element_type=jnp.float32) * scaling
    )
    scores = jnp.where(same_window[None], scores, -1e30)
    weights = softmax_rows(scores).astype(jnp.bfloat16)
    return jnp.einsum(
        "hst,thd->shd", weights, value_rows, preferred_element_type=jnp.float32
    ).astype(jnp.bfloat16)


def gather_body(queries, keys, values, head_class, window_lengths, out_weight):
    tok_len, columns = queries.shape
    local_heads = columns // HD
    scaling = 1.0 / math.sqrt(HD)
    head_group = lax.axis_index("head")
    classes = lax.dynamic_slice_in_dim(head_class, head_group * local_heads, local_heads)
    temporal_mask = classes == 1
    slot_rank = jnp.cumsum(temporal_mask.astype(jnp.int32)) - 1
    slot_ids = jnp.arange(TMAX, dtype=jnp.int32)
    picker = ((slot_rank[None, :] == slot_ids[:, None]) & temporal_mask[None, :]).astype(
        jnp.bfloat16
    )
    shaped = [array_in.reshape(tok_len, local_heads, HD) for array_in in (queries, keys, values)]
    lengths = window_lengths[0]
    spatial_out = window_attention(shaped[0], shaped[1], shaped[2], lengths, scaling)
    packed = [compact_heads(array_in, picker)[None] for array_in in shaped]
    query = lax.all_to_all(packed[0], "seq", split_axis=1, concat_axis=0, tiled=True)
    key_rows = lax.all_to_all(packed[1], "seq", split_axis=1, concat_axis=0, tiled=True)
    value_rows = lax.all_to_all(packed[2], "seq", split_axis=1, concat_axis=0, tiled=True)
    sources, width, count, size = query.shape
    groups = sources // FRAMES
    query = query.reshape(FRAMES, groups, width, count, size)
    key_rows = key_rows.reshape(FRAMES, groups, width, count, size)
    value_rows = value_rows.reshape(FRAMES, groups, width, count, size)
    scores = (
        jnp.einsum("fjcnd,gjcnd->jcnfg", query, key_rows, preferred_element_type=jnp.float32)
        * scaling
    )
    weights = softmax_rows(scores).astype(jnp.bfloat16)
    attended = jnp.einsum(
        "jcnfg,gjcnd->fjcnd", weights, value_rows, preferred_element_type=jnp.float32
    ).astype(jnp.bfloat16)
    attended = attended.reshape(sources, width, count, size)
    returned = lax.all_to_all(attended, "seq", split_axis=0, concat_axis=1, tiled=True)
    temporal_out = expand_heads(returned[0], picker)
    mixed = jnp.where(temporal_mask[None, :, None], temporal_out, spatial_out)
    mixed_local = mixed.reshape(tok_len, local_heads * HD)
    mixed_all = lax.all_gather(mixed_local, "head", axis=1, tiled=True)
    summed = jnp.dot(
        mixed_all,
        lax.all_gather(out_weight, "seq", axis=0, tiled=True),
        preferred_element_type=jnp.float32,
    )
    return summed.astype(jnp.bfloat16)


MESH = pl.DeviceIdType.MESH
CHUNKS = 5
EARLY = 2
VMEM_LIMIT = 62 * 1024 * 1024


def masked_attention(triples, same, scaling):
    scores = [
        lax.dot_general(q, k, (((1,), (1,)), ((), ())), preferred_element_type=jnp.float32)
        for q, k, _ in triples
    ]
    scores = [jnp.where(same, score * scaling, -1e30) for score in scores]
    highest = [jnp.max(score, axis=-1, keepdims=True) for score in scores]
    weights = [jnp.exp(score - top) for score, top in zip(scores, highest)]
    totals = [jnp.sum(weight, axis=-1, keepdims=True) for weight in weights]
    weights = [(weight / total).astype(jnp.bfloat16) for weight, total in zip(weights, totals)]
    return [
        jnp.dot(weight, v, preferred_element_type=jnp.float32).astype(jnp.bfloat16)
        for weight, (_, _, v) in zip(weights, triples)
    ]


def slot_conditions(class_ref, first, local_heads):
    rank = jnp.int32(0)
    taken = []
    for h in range(local_heads):
        flag = (class_ref[first + h] == 1).astype(jnp.int32)
        taken.append([flag * (rank == t).astype(jnp.int32) == 1 for t in range(TMAX)])
        rank = rank + flag
    return taken


def layer_kernel(
    n, groups, class_hbm, len_hbm, q_hbm, k_hbm, v_hbm, w_ref, out_ref,
    class_ref, len_ref, q_ref, k_ref, v_ref,
    packed, landed, spat, spat_in, tsend, temp_in, mixed, w_all, partial,
    up_in, up_out, down_in, down_out,
    load_s, qkv_s, qkv_r, w_s, w_r, w_l, sp_s, sp_r, share_s, share_r, t_s, t_r,
    up_s, up_r, down_s, down_r,
):
    pair = n // groups
    seq, head = lax.axis_index("seq"), lax.axis_index("head")
    plane, lane = seq // pair, lax.rem(seq, pair)
    rank = lane * groups + head
    core = lax.rem(head, 2)
    sibling = head + 1 - 2 * core
    across = lax.rem(head + groups // 2, groups)
    at_home = plane == head
    tok, columns = q_ref.shape
    local_heads = columns // HD
    width, quarter = tok // n, tok // groups
    rows = w_ref.shape[0]
    chunk = w_ref.shape[1] // CHUNKS
    scaling = 1.0 / math.sqrt(HD)

    def send(src, dst, send_sem, recv_sem, to_seq, to_head):
        return pltpu.make_async_remote_copy(
            src_ref=src, dst_ref=dst, send_sem=send_sem, recv_sem=recv_sem,
            device_id=(to_seq, to_head), device_id_type=MESH,
        )

    loads = [
        pltpu.make_async_copy(src, dst, load_s.at[i])
        for i, (src, dst) in enumerate(
            ((class_hbm, class_ref), (q_hbm, q_ref), (k_hbm, k_ref), (v_hbm, v_ref), (len_hbm, len_ref))
        )
    ]
    for load in loads:
        load.start()
    own_w = pltpu.make_async_copy(w_ref, w_all.at[lane], w_l)
    own_w.start()

    barrier = pltpu.get_barrier_semaphore()

    def greet(to_seq, to_head):
        pl.semaphore_signal(barrier, inc=1, device_id=(to_seq, to_head), device_id_type=MESH)

    for step in range(1, n):
        other = lax.rem(rank + step, n)
        greet(plane * pair + other // groups, lax.rem(other, groups))
    for step in range(1, groups):
        for x in range(pair):
            greet(lax.rem(plane + step, groups) * pair + x, plane)

    @pl.when(plane > 0)
    def _():
        greet(seq - pair, head)

    @pl.when(plane < groups - 1)
    def _():
        greet(seq + pair, head)

    for load in loads[:4]:
        load.wait()

    taken = slot_conditions(class_ref, head * local_heads, local_heads)
    for a, ref in enumerate((q_ref, k_ref, v_ref)):
        for t in range(TMAX):
            value = jnp.zeros((tok, HD), jnp.bfloat16)
            for h in range(t, local_heads):
                value = jnp.where(taken[h][t], ref[:, h * HD:(h + 1) * HD], value)
            at = (a * TMAX + t) * HD
            packed[:, :, at:at + HD] = value.reshape(n, width, HD)

    @pl.when(plane == 0)
    def _():
        up_in[...] = jnp.zeros_like(up_in)

    @pl.when(plane == groups - 1)
    def _():
        down_in[...] = jnp.zeros_like(down_in)

    greeted = n - 1 + (plane > 0).astype(jnp.int32) + (plane < groups - 1).astype(jnp.int32)
    pl.semaphore_wait(barrier, greeted + n * jnp.logical_not(at_home).astype(jnp.int32))

    def qkv_copy(step):
        to = lax.rem(rank + step, n)
        return send(
            packed.at[to], landed.at[seq], qkv_s.at[to], qkv_r.at[seq],
            head * pair + to // groups, lax.rem(to, groups),
        )

    for step in range(1, n):
        qkv_copy(step).start()

    @pl.when(jnp.logical_not(at_home))
    def _():
        qkv_copy(0).start()

    @pl.when(at_home)
    def _():
        landed[seq] = packed[rank]

    def w_copy(c, owner):
        cols = pl.ds(c * chunk, chunk)
        return send(
            w_ref.at[:, cols], w_all.at[owner, :, cols], w_s.at[c], w_r.at[c],
            plane * pair + (1 - lane), head,
        )

    for c in range(EARLY):
        w_copy(c, lane).start()

    loads[4].wait()

    def window_of(axis):
        position = lax.broadcasted_iota(jnp.int32, (tok, tok), axis)
        ids = jnp.zeros((tok, tok), jnp.int32)
        end = jnp.int32(0)
        for i in range(len_ref.shape[1]):
            end = end + len_ref[0, i]
            ids = ids + (position >= end).astype(jnp.int32)
        return ids

    same_window = window_of(0) == window_of(1)
    spans = [slice(h * HD, (h + 1) * HD) for h in range(local_heads)]
    results = masked_attention(
        [(q_ref[:, at], k_ref[:, at], v_ref[:, at]) for at in spans], same_window, scaling
    )
    for at, value in zip(spans, results):
        spat[:, :, at] = value.reshape(groups, quarter, HD)

    def spatial_copy(step):
        to = lax.rem(head + step, groups)
        return send(
            spat.at[to], spat_in.at[to, plane], sp_s.at[to], sp_r.at[plane], head * pair + lane, to
        )

    for step in range(1, groups):
        spatial_copy(step).start()

    @pl.when(jnp.logical_not(at_home))
    def _():
        spatial_copy(0).start()

    @pl.when(at_home)
    def _():
        spat_in[head, plane] = spat[head]

    for source in range(n):
        @pl.when(jnp.logical_not(at_home & (seq == source)))
        def _(source=source):
            send(
                landed.at[source], landed.at[source], qkv_s.at[source], qkv_r.at[source], seq, head
            ).wait_recv()

    for z in range(groups):
        @pl.when(jnp.logical_not(at_home & (plane == z)))
        def _(z=z):
            send(
                spat.at[z], spat_in.at[head, z], sp_s.at[z], sp_r.at[z], seq, head
            ).wait_recv()

    def share(which, slot, to_head):
        return send(spat_in.at[which], spat_in.at[which], share_s.at[slot], share_r.at[which], seq, to_head)

    share(head, 0, across).start()
    share(head, 1, sibling).start()

    row = lax.rem(lax.broadcasted_iota(jnp.int32, (tok, tok), 0), width)
    column = lax.rem(lax.broadcasted_iota(jnp.int32, (tok, tok), 1), width)
    same_position = row == column
    triples = [
        tuple(
            landed[:, :, (a * TMAX + t) * HD:(a * TMAX + t + 1) * HD].reshape(tok, HD)
            for a in range(3)
        )
        for t in range(TMAX)
    ]
    for t, result in enumerate(masked_attention(triples, same_position, scaling)):
        for f in range(n):
            tsend[f % pair, f // pair, :, t * HD:(t + 1) * HD] = result[f * width:(f + 1) * width]

    def temporal_copy(step):
        to = lax.rem(rank + step, n)
        x = to // groups
        return send(
            tsend.at[x], temp_in.at[rank], t_s.at[to], t_r.at[rank], plane * pair + x, lax.rem(to, groups)
        )

    for step in range(1, n):
        temporal_copy(step).start()
    temp_in[rank] = tsend[lane]
    for c in range(EARLY, CHUNKS):
        w_copy(c, lane).start()

    share(across, 0, across).wait_recv()
    share(across, 2, sibling).start()
    share(sibling, 1, sibling).wait_recv()
    share(lax.rem(sibling + groups // 2, groups), 2, sibling).wait_recv()
    for step in range(1, n):
        source = lax.rem(rank + n - step, n)
        send(
            temp_in.at[source], temp_in.at[source], t_s.at[source], t_r.at[source], seq, head
        ).wait_recv()

    taken = slot_conditions(class_ref, plane * local_heads, local_heads)
    for z in range(groups):
        for h in range(local_heads):
            value = spat_in[:, z, :, h * HD:(h + 1) * HD].reshape(tok, HD)
            for t in range(min(h + 1, TMAX)):
                slot = temp_in[:, z, :, t * HD:(t + 1) * HD].reshape(tok, HD)
                value = jnp.where(taken[h][t], slot, value)
            mixed[z, :, h * HD:(h + 1) * HD] = value

    own_w.wait()

    def multiply(c):
        w_copy(c, 1 - lane).wait_recv()
        weight = w_all[:, :, c * chunk:(c + 1) * chunk].reshape(pair * rows, chunk)
        result = jnp.dot(
            mixed[...].reshape(groups * tok, columns), weight, preferred_element_type=jnp.float32
        )
        partial[c] = result.reshape(groups, tok, chunk)

    ways = ((1, up_in, up_out, up_s, up_r), (-1, down_in, down_out, down_s, down_r))

    def onward(way, d, c):
        sign, came, goes, s_sem, r_sem = way
        to_seq = seq + sign * pair
        return send(goes.at[d - 1, c], came.at[d - 1, c], s_sem.at[d - 1, c], r_sem.at[d - 1, c], to_seq, head)

    def has_previous(way):
        return plane > 0 if way[0] == 1 else plane < groups - 1

    def reaches(way, d):
        return plane + d < groups if way[0] == 1 else plane >= d

    def arrive(way, d, c):
        @pl.when(has_previous(way))
        def _():
            sign, came, goes, s_sem, r_sem = way
            send(goes.at[d, c], came.at[d, c], s_sem.at[d, c], r_sem.at[d, c], seq, head).wait_recv()

    for c in range(CHUNKS):
        multiply(c)
        for d in range(groups - 1, 0, -1):
            for way in ways:
                @pl.when(reaches(way, d))
                def _(way=way, d=d, c=c):
                    total = partial[c, plane + way[0] * d]
                    if d < groups - 1:
                        arrive(way, d, c)
                        total = total + way[1][d, c].astype(jnp.float32)
                    way[2][d - 1, c] = total.astype(jnp.bfloat16)
                    onward(way, d, c).start()
    for c in range(CHUNKS):
        total = partial[c, plane]
        for way in ways:
            arrive(way, 0, c)
            total = total + way[1][0, c].astype(jnp.float32)
        out_ref[:, c * chunk:(c + 1) * chunk] = total.astype(jnp.bfloat16)

    @pl.when(jnp.logical_not(at_home))
    def _():
        qkv_copy(0).wait_send()
        spatial_copy(0).wait_send()

    for step in range(1, n):
        qkv_copy(step).wait_send()
        temporal_copy(step).wait_send()
    for step in range(1, groups):
        spatial_copy(step).wait_send()
    share(head, 0, across).wait_send()
    share(head, 1, sibling).wait_send()
    share(across, 2, sibling).wait_send()
    for c in range(CHUNKS):
        w_copy(c, lane).wait_send()
    for d in range(groups - 1, 0, -1):
        for c in range(CHUNKS):
            for way in ways:
                @pl.when(reaches(way, d))
                def _(way=way, d=d, c=c):
                    onward(way, d, c).wait_send()


def kernel_body(n, groups, queries, keys, values, head_class, window_lengths, out_weight):
    tok, columns = queries.shape
    rows, out_columns = out_weight.shape
    pair, width, quarter = n // groups, tok // n, tok // groups
    chunk = out_columns // CHUNKS
    bf16, dma = jnp.bfloat16, pltpu.SemaphoreType.DMA
    line = (groups - 1, CHUNKS)
    return pl.pallas_call(
        functools.partial(layer_kernel, n, groups),
        out_shape=jax.ShapeDtypeStruct((tok, out_columns), bf16),
        in_specs=[pl.BlockSpec(memory_space=pl.ANY)] * 6,
        out_specs=pl.BlockSpec(memory_space=pltpu.VMEM),
        scratch_shapes=[
            pltpu.SMEM(head_class.shape, jnp.int32),
            pltpu.SMEM(window_lengths.shape, jnp.int32),
            pltpu.VMEM((tok, columns), bf16),
            pltpu.VMEM((tok, columns), bf16),
            pltpu.VMEM((tok, columns), bf16),
            pltpu.VMEM((n, width, 3 * TMAX * HD), bf16),
            pltpu.VMEM((n, width, 3 * TMAX * HD), bf16),
            pltpu.VMEM((groups, quarter, columns), bf16),
            pltpu.VMEM((groups, groups, quarter, columns), bf16),
            pltpu.VMEM((pair, groups, width, TMAX * HD), bf16),
            pltpu.VMEM((n, groups, width, TMAX * HD), bf16),
            pltpu.VMEM((groups, tok, columns), bf16),
            pltpu.VMEM((pair, rows, out_columns), bf16),
            pltpu.VMEM((CHUNKS, groups, tok, chunk), jnp.float32),
            pltpu.VMEM(line + (tok, chunk), bf16),
            pltpu.VMEM(line + (tok, chunk), bf16),
            pltpu.VMEM(line + (tok, chunk), bf16),
            pltpu.VMEM(line + (tok, chunk), bf16),
            dma((5,)), dma((n,)), dma((n,)),
            dma((CHUNKS,)), dma((CHUNKS,)), dma,
            dma((groups,)), dma((groups,)), dma((3,)), dma((groups,)),
            dma((n,)), dma((n,)),
            dma(line), dma(line), dma(line), dma(line),
        ],
        compiler_params=pltpu.CompilerParams(
            collective_id=0, has_side_effects=True, vmem_limit_bytes=VMEM_LIMIT
        ),
        cost_estimate=pl.CostEstimate(
            flops=2 * groups * tok * columns * out_columns,
            bytes_accessed=4 * rows * out_columns,
            transcendentals=local_count(columns) * tok * tok,
        ),
    )(head_class, window_lengths, queries, keys, values, out_weight)


def local_count(columns):
    return columns // HD + TMAX


def solution(mesh):
    n, groups = mesh.shape["seq"], mesh.shape["head"]

    def body(queries, keys, values, head_class, window_lengths, out_weight):
        tok, rows = queries.shape[0], out_weight.shape[0]
        if n == FRAMES and n == 2 * groups and rows > tok:
            return kernel_body(
                n, groups, queries, keys, values, head_class, window_lengths, out_weight
            )
        return gather_body(queries, keys, values, head_class, window_lengths, out_weight)

    placed = (
        P("seq", "head"),
        P("seq", "head"),
        P("seq", "head"),
        P(),
        P("seq", None),
        P("seq", "head"),
    )
    return jax.shard_map(
        body, mesh=mesh, in_specs=placed, out_specs=P("seq", "head"), check_vma=False
    )
```

```python
import functools
import math

import jax
import jax.numpy as jnp
from jax import lax
from jax.experimental import pallas as pl
from jax.experimental.pallas import tpu as pltpu
from jax.sharding import PartitionSpec as P

HD = 128
TMAX = 3
FRAMES = 8


def softmax_rows(scores):
    highest = jnp.max(scores, axis=-1, keepdims=True)
    weights = jnp.exp(scores - highest)
    return weights / jnp.sum(weights, axis=-1, keepdims=True)


def compact_heads(source, picker):
    return jnp.einsum("shd,th->std", source, picker, preferred_element_type=jnp.float32).astype(
        jnp.bfloat16
    )


def expand_heads(source, picker):
    return jnp.einsum("std,th->shd", source, picker, preferred_element_type=jnp.float32).astype(
        jnp.bfloat16
    )


def window_attention(query, key_rows, value_rows, lengths, scaling):
    ends = jnp.cumsum(lengths)
    positions = jnp.arange(query.shape[0], dtype=jnp.int32)
    window_ids = jnp.sum((positions[:, None] >= ends[None, :]).astype(jnp.int32), axis=1)
    same_window = window_ids[:, None] == window_ids[None, :]
    scores = (
        jnp.einsum("shd,thd->hst", query, key_rows, preferred_element_type=jnp.float32) * scaling
    )
    scores = jnp.where(same_window[None], scores, -1e30)
    weights = softmax_rows(scores).astype(jnp.bfloat16)
    return jnp.einsum(
        "hst,thd->shd", weights, value_rows, preferred_element_type=jnp.float32
    ).astype(jnp.bfloat16)


def gather_body(queries, keys, values, head_class, window_lengths, out_weight):
    tok_len, columns = queries.shape
    local_heads = columns // HD
    scaling = 1.0 / math.sqrt(HD)
    head_group = lax.axis_index("head")
    classes = lax.dynamic_slice_in_dim(head_class, head_group * local_heads, local_heads)
    temporal_mask = classes == 1
    slot_rank = jnp.cumsum(temporal_mask.astype(jnp.int32)) - 1
    slot_ids = jnp.arange(TMAX, dtype=jnp.int32)
    picker = ((slot_rank[None, :] == slot_ids[:, None]) & temporal_mask[None, :]).astype(
        jnp.bfloat16
    )
    shaped = [array_in.reshape(tok_len, local_heads, HD) for array_in in (queries, keys, values)]
    lengths = window_lengths[0]
    spatial_out = window_attention(shaped[0], shaped[1], shaped[2], lengths, scaling)
    packed = [compact_heads(array_in, picker)[None] for array_in in shaped]
    query = lax.all_to_all(packed[0], "seq", split_axis=1, concat_axis=0, tiled=True)
    key_rows = lax.all_to_all(packed[1], "seq", split_axis=1, concat_axis=0, tiled=True)
    value_rows = lax.all_to_all(packed[2], "seq", split_axis=1, concat_axis=0, tiled=True)
    sources, width, count, size = query.shape
    groups = sources // FRAMES
    query = query.reshape(FRAMES, groups, width, count, size)
    key_rows = key_rows.reshape(FRAMES, groups, width, count, size)
    value_rows = value_rows.reshape(FRAMES, groups, width, count, size)
    scores = (
        jnp.einsum("fjcnd,gjcnd->jcnfg", query, key_rows, preferred_element_type=jnp.float32)
        * scaling
    )
    weights = softmax_rows(scores).astype(jnp.bfloat16)
    attended = jnp.einsum(
        "jcnfg,gjcnd->fjcnd", weights, value_rows, preferred_element_type=jnp.float32
    ).astype(jnp.bfloat16)
    attended = attended.reshape(sources, width, count, size)
    returned = lax.all_to_all(attended, "seq", split_axis=0, concat_axis=1, tiled=True)
    temporal_out = expand_heads(returned[0], picker)
    mixed = jnp.where(temporal_mask[None, :, None], temporal_out, spatial_out)
    mixed_local = mixed.reshape(tok_len, local_heads * HD)
    mixed_all = lax.all_gather(mixed_local, "head", axis=1, tiled=True)
    summed = jnp.dot(
        mixed_all,
        lax.all_gather(out_weight, "seq", axis=0, tiled=True),
        preferred_element_type=jnp.float32,
    )
    return summed.astype(jnp.bfloat16)


MESH = pl.DeviceIdType.MESH
CHUNKS = 2
VMEM_LIMIT = 62 * 1024 * 1024


def masked_attention(triples, same, scaling):
    scores = [
        lax.dot_general(q, k, (((1,), (1,)), ((), ())), preferred_element_type=jnp.float32)
        for q, k, _ in triples
    ]
    scores = [jnp.where(same, score * scaling, -1e30) for score in scores]
    highest = [jnp.max(score, axis=-1, keepdims=True) for score in scores]
    weights = [jnp.exp(score - top) for score, top in zip(scores, highest)]
    totals = [jnp.sum(weight, axis=-1, keepdims=True) for weight in weights]
    weights = [(weight / total).astype(jnp.bfloat16) for weight, total in zip(weights, totals)]
    return [
        jnp.dot(weight, v, preferred_element_type=jnp.float32).astype(jnp.bfloat16)
        for weight, (_, _, v) in zip(weights, triples)
    ]


def slot_conditions(class_ref, first, local_heads):
    rank = jnp.int32(0)
    taken = []
    for h in range(local_heads):
        flag = (class_ref[first + h] == 1).astype(jnp.int32)
        taken.append([flag * (rank == t).astype(jnp.int32) == 1 for t in range(TMAX)])
        rank = rank + flag
    return taken


def layer_kernel(
    n, groups, class_hbm, len_hbm, q_hbm, k_hbm, v_hbm, w_ref, out_ref,
    class_ref, len_ref, q_ref, k_ref, v_ref,
    packed, landed, spat, spat_in, tsend, temp_in, mixed, w_all, partial,
    up_in, up_out, down_in, down_out,
    load_s, qkv_s, qkv_r, w_s, w_r, w_l, sp_s, sp_r, sp_l, spf_s, t_s, t_r, t_l, tf_s,
    up_s, up_r, down_s, down_r,
):
    pair = n // groups
    seq, head = lax.axis_index("seq"), lax.axis_index("head")
    plane, lane = seq // pair, lax.rem(seq, pair)
    core = lax.rem(head, 2)
    sibling = head + 1 - 2 * core
    tok, columns = q_ref.shape
    local_heads = columns // HD
    width = tok // n
    rows = w_ref.shape[0]
    scaling = 1.0 / math.sqrt(HD)

    def send(src, dst, send_sem, recv_sem, to_seq, to_head):
        return pltpu.make_async_remote_copy(
            src_ref=src, dst_ref=dst, send_sem=send_sem, recv_sem=recv_sem,
            device_id=(to_seq, to_head), device_id_type=MESH,
        )

    loads = [
        pltpu.make_async_copy(src, dst, load_s.at[i])
        for i, (src, dst) in enumerate(
            ((class_hbm, class_ref), (q_hbm, q_ref), (k_hbm, k_ref), (v_hbm, v_ref), (len_hbm, len_ref))
        )
    ]
    for load in loads:
        load.start()
    own_w = pltpu.make_async_copy(w_ref, w_all.at[lane], w_l)
    own_w.start()

    barrier = pltpu.get_barrier_semaphore()

    def greet(to_seq, to_head):
        pl.semaphore_signal(barrier, inc=1, device_id=(to_seq, to_head), device_id_type=MESH)

    for step in range(1, n):
        greet(lax.rem(seq + step, n), head)
    greet(seq, sibling)

    @pl.when(plane != head)
    def _():
        for peer in range(n):
            greet(jnp.int32(peer), plane)

    for load in loads[:4]:
        load.wait()

    taken = slot_conditions(class_ref, head * local_heads, local_heads)
    for a, ref in enumerate((q_ref, k_ref, v_ref)):
        for t in range(TMAX):
            value = jnp.zeros((tok, HD), jnp.bfloat16)
            for h in range(t, local_heads):
                value = jnp.where(taken[h][t], ref[:, h * HD:(h + 1) * HD], value)
            at = (a * TMAX + t) * HD
            packed[:, :, at:at + HD] = value.reshape(n, width, HD)

    @pl.when(plane == 0)
    def _():
        up_in[...] = jnp.zeros_like(up_in)

    @pl.when(plane == groups - 1)
    def _():
        down_in[...] = jnp.zeros_like(down_in)

    pl.semaphore_wait(barrier, (n - 1) + pair * (groups - 1) + 1)

    qkv = []
    for step in range(1, n):
        peer = lax.rem(seq + step, n)
        copy = send(packed.at[peer], landed.at[seq], qkv_s.at[peer], qkv_r.at[seq], peer, head)
        copy.start()
        qkv.append(copy)
    landed[seq] = packed[seq]

    other = plane * pair + (1 - lane)
    w_copy = send(w_ref, w_all.at[lane], w_s, w_r.at[lane], other, head)
    w_copy.start()

    loads[4].wait()
    def window_of(axis):
        position = lax.broadcasted_iota(jnp.int32, (tok, tok), axis)
        ids = jnp.zeros((tok, tok), jnp.int32)
        end = jnp.int32(0)
        for i in range(len_ref.shape[1]):
            end = end + len_ref[0, i]
            ids = ids + (position >= end).astype(jnp.int32)
        return ids

    same_window = window_of(0) == window_of(1)
    spans = [slice(h * HD, (h + 1) * HD) for h in range(local_heads)]
    results = masked_attention(
        [(q_ref[:, at], k_ref[:, at], v_ref[:, at]) for at in spans], same_window, scaling
    )
    for at, value in zip(spans, results):
        spat[:, at] = value

    sp_core = lax.rem(plane, 2)
    sp_copies = []
    for y in range(groups // 2):
        to_seq, to_head = head * pair + lane, 2 * y + sp_core
        mine = (to_seq == seq) & (to_head == head)
        copy = send(spat, spat_in.at[plane], sp_s.at[y], sp_r.at[plane], to_seq, to_head)
        sp_copies.append((mine, copy))

        @pl.when(jnp.logical_not(mine))
        def _(copy=copy):
            copy.start()

        @pl.when(mine)
        def _():
            spat_in[plane] = spat[...]

    for step in range(1, n):
        peer = lax.rem(seq + n - step, n)
        send(landed.at[peer], landed.at[peer], qkv_s.at[peer], qkv_r.at[peer], peer, head).wait_recv()
    row = lax.rem(lax.broadcasted_iota(jnp.int32, (tok, tok), 0), width)
    column = lax.rem(lax.broadcasted_iota(jnp.int32, (tok, tok), 1), width)
    same_position = row == column
    triples = [
        tuple(
            landed[:, :, (a * TMAX + t) * HD:(a * TMAX + t + 1) * HD].reshape(tok, HD)
            for a in range(3)
        )
        for t in range(TMAX)
    ]
    for t, result in enumerate(masked_attention(triples, same_position, scaling)):
        for f in range(n):
            tsend[f % pair, f // pair, :, t * HD:(t + 1) * HD] = result[f * width:(f + 1) * width]

    t_core = lax.rem(seq, 2)
    t_copies = []
    for x in range(pair):
        for y in range(groups // 2):
            to_seq, to_head = head * pair + x, 2 * y + t_core
            mine = (to_seq == seq) & (to_head == head)
            copy = send(tsend.at[x], temp_in.at[seq], t_s.at[x, y], t_r.at[seq], to_seq, to_head)
            t_copies.append((mine, copy))

            @pl.when(jnp.logical_not(mine))
            def _(copy=copy):
                copy.start()

            @pl.when(mine)
            def _(x=x):
                temp_in[seq] = tsend[x]

    forwards = []
    for j in range(groups // 2):
        source = 2 * j + core
        here = (source == plane) & (plane == head)
        copy = send(spat_in.at[source], spat_in.at[source], spf_s.at[j], sp_r.at[source], seq, sibling)

        @pl.when(jnp.logical_not(here))
        def _(copy=copy):
            copy.wait_recv()

        copy.start()
        forwards.append(copy)
    for j in range(n // 2):
        source = 2 * j + core
        here = (source == seq) & (plane == head)
        copy = send(temp_in.at[source], temp_in.at[source], tf_s.at[j], t_r.at[source], seq, sibling)

        @pl.when(jnp.logical_not(here))
        def _(copy=copy):
            copy.wait_recv()

        copy.start()
        forwards.append(copy)
    for j in range(groups // 2):
        source = 2 * j + 1 - core
        send(spat_in.at[source], spat_in.at[source], spf_s.at[j], sp_r.at[source], seq, sibling).wait_recv()
    for j in range(n // 2):
        source = 2 * j + 1 - core
        send(temp_in.at[source], temp_in.at[source], tf_s.at[j], t_r.at[source], seq, sibling).wait_recv()

    taken = slot_conditions(class_ref, plane * local_heads, local_heads)
    for z in range(groups):
        for h in range(local_heads):
            value = spat_in[z, :, h * HD:(h + 1) * HD]
            for t in range(min(h + 1, TMAX)):
                slot = temp_in[:, z, :, t * HD:(t + 1) * HD].reshape(tok, HD)
                value = jnp.where(taken[h][t], slot, value)
            mixed[z, :, h * HD:(h + 1) * HD] = value

    own_w.wait()
    send(w_ref, w_all.at[1 - lane], w_s, w_r.at[1 - lane], other, head).wait_recv()

    chunk = w_ref.shape[1] // CHUNKS

    def multiply(c):
        weight = w_all[:, :, c * chunk:(c + 1) * chunk].reshape(pair * rows, chunk)
        result = jnp.dot(
            mixed[...].reshape(groups * tok, columns), weight, preferred_element_type=jnp.float32
        )
        partial[c] = result.reshape(groups, tok, chunk)

    ways = ((1, up_in, up_out, up_s, up_r), (-1, down_in, down_out, down_s, down_r))

    def onward(way, d, c):
        sign, came, goes, s_sem, r_sem = way
        to_seq = seq + sign * pair
        return send(goes.at[d - 1, c], came.at[d - 1, c], s_sem.at[d - 1, c], r_sem.at[d - 1, c], to_seq, head)

    def has_previous(way):
        return plane > 0 if way[0] == 1 else plane < groups - 1

    def reaches(way, d):
        return plane + d < groups if way[0] == 1 else plane >= d

    def arrive(way, d, c):
        @pl.when(has_previous(way))
        def _():
            sign, came, goes, s_sem, r_sem = way
            send(goes.at[d, c], came.at[d, c], s_sem.at[d, c], r_sem.at[d, c], seq, head).wait_recv()

    for d in range(groups - 1, 0, -1):
        for c in range(CHUNKS):
            if d == groups - 1:
                multiply(c)
            for way in ways:
                @pl.when(reaches(way, d))
                def _(way=way, d=d, c=c):
                    total = partial[c, plane + way[0] * d]
                    if d < groups - 1:
                        arrive(way, d, c)
                        total = total + way[1][d, c].astype(jnp.float32)
                    way[2][d - 1, c] = total.astype(jnp.bfloat16)
                    onward(way, d, c).start()
    for c in range(CHUNKS):
        total = partial[c, plane]
        for way in ways:
            arrive(way, 0, c)
            total = total + way[1][0, c].astype(jnp.float32)
        out_ref[:, c * chunk:(c + 1) * chunk] = total.astype(jnp.bfloat16)

    for copy in qkv:
        copy.wait_send()
    w_copy.wait_send()
    for mine, copy in sp_copies + t_copies:
        @pl.when(jnp.logical_not(mine))
        def _(copy=copy):
            copy.wait_send()
    for copy in forwards:
        copy.wait_send()
    for d in range(groups - 1, 0, -1):
        for c in range(CHUNKS):
            for way in ways:
                @pl.when(reaches(way, d))
                def _(way=way, d=d, c=c):
                    onward(way, d, c).wait_send()


def kernel_body(n, groups, queries, keys, values, head_class, window_lengths, out_weight):
    tok, columns = queries.shape
    rows, out_columns = out_weight.shape
    pair, width = n // groups, tok // n
    chunk = out_columns // CHUNKS
    bf16, dma = jnp.bfloat16, pltpu.SemaphoreType.DMA
    line = (groups - 1, CHUNKS)
    return pl.pallas_call(
        functools.partial(layer_kernel, n, groups),
        out_shape=jax.ShapeDtypeStruct((tok, out_columns), bf16),
        in_specs=[pl.BlockSpec(memory_space=pl.ANY)] * 6,
        out_specs=pl.BlockSpec(memory_space=pltpu.VMEM),
        scratch_shapes=[
            pltpu.SMEM(head_class.shape, jnp.int32),
            pltpu.SMEM(window_lengths.shape, jnp.int32),
            pltpu.VMEM((tok, columns), bf16),
            pltpu.VMEM((tok, columns), bf16),
            pltpu.VMEM((tok, columns), bf16),
            pltpu.VMEM((n, width, 3 * TMAX * HD), bf16),
            pltpu.VMEM((n, width, 3 * TMAX * HD), bf16),
            pltpu.VMEM((tok, columns), bf16),
            pltpu.VMEM((groups, tok, columns), bf16),
            pltpu.VMEM((pair, groups, width, TMAX * HD), bf16),
            pltpu.VMEM((n, groups, width, TMAX * HD), bf16),
            pltpu.VMEM((groups, tok, columns), bf16),
            pltpu.VMEM((pair, rows, out_columns), bf16),
            pltpu.VMEM((CHUNKS, groups, tok, chunk), jnp.float32),
            pltpu.VMEM(line + (tok, chunk), bf16),
            pltpu.VMEM(line + (tok, chunk), bf16),
            pltpu.VMEM(line + (tok, chunk), bf16),
            pltpu.VMEM(line + (tok, chunk), bf16),
            dma((5,)), dma((n,)), dma((n,)),
            dma, dma((pair,)), dma,
            dma((groups // 2,)), dma((groups,)), dma, dma((groups // 2,)),
            dma((pair, groups // 2)), dma((n,)), dma, dma((n // 2,)),
            dma(line), dma(line), dma(line), dma(line),
        ],
        compiler_params=pltpu.CompilerParams(
            collective_id=0, has_side_effects=True, vmem_limit_bytes=VMEM_LIMIT
        ),
        cost_estimate=pl.CostEstimate(
            flops=2 * groups * tok * columns * out_columns,
            bytes_accessed=4 * rows * out_columns,
            transcendentals=local_count(columns) * tok * tok,
        ),
    )(head_class, window_lengths, queries, keys, values, out_weight)


def local_count(columns):
    return columns // HD + TMAX


def solution(mesh):
    n, groups = mesh.shape["seq"], mesh.shape["head"]

    def body(queries, keys, values, head_class, window_lengths, out_weight):
        tok, rows = queries.shape[0], out_weight.shape[0]
        if n == FRAMES and n == 2 * groups and rows > tok:
            return kernel_body(
                n, groups, queries, keys, values, head_class, window_lengths, out_weight
            )
        return gather_body(queries, keys, values, head_class, window_lengths, out_weight)

    placed = (
        P("seq", "head"),
        P("seq", "head"),
        P("seq", "head"),
        P(),
        P("seq", None),
        P("seq", "head"),
    )
    return jax.shard_map(
        body, mesh=mesh, in_specs=placed, out_specs=P("seq", "head"), check_vma=False
    )
```

```python
import functools
import math

import jax
import jax.numpy as jnp
from jax import lax
from jax.experimental import pallas as pl
from jax.experimental.pallas import tpu as pltpu
from jax.sharding import PartitionSpec as P

HD = 128
TMAX = 3
FRAMES = 8


def softmax_rows(scores):
    highest = jnp.max(scores, axis=-1, keepdims=True)
    weights = jnp.exp(scores - highest)
    return weights / jnp.sum(weights, axis=-1, keepdims=True)


def compact_heads(source, picker):
    return jnp.einsum("shd,th->std", source, picker, preferred_element_type=jnp.float32).astype(
        jnp.bfloat16
    )


def expand_heads(source, picker):
    return jnp.einsum("std,th->shd", source, picker, preferred_element_type=jnp.float32).astype(
        jnp.bfloat16
    )


def window_attention(query, key_rows, value_rows, lengths, scaling):
    ends = jnp.cumsum(lengths)
    positions = jnp.arange(query.shape[0], dtype=jnp.int32)
    window_ids = jnp.sum((positions[:, None] >= ends[None, :]).astype(jnp.int32), axis=1)
    same_window = window_ids[:, None] == window_ids[None, :]
    scores = (
        jnp.einsum("shd,thd->hst", query, key_rows, preferred_element_type=jnp.float32) * scaling
    )
    scores = jnp.where(same_window[None], scores, -1e30)
    weights = softmax_rows(scores).astype(jnp.bfloat16)
    return jnp.einsum(
        "hst,thd->shd", weights, value_rows, preferred_element_type=jnp.float32
    ).astype(jnp.bfloat16)


def gather_body(queries, keys, values, head_class, window_lengths, out_weight):
    tok_len, columns = queries.shape
    local_heads = columns // HD
    scaling = 1.0 / math.sqrt(HD)
    head_group = lax.axis_index("head")
    classes = lax.dynamic_slice_in_dim(head_class, head_group * local_heads, local_heads)
    temporal_mask = classes == 1
    slot_rank = jnp.cumsum(temporal_mask.astype(jnp.int32)) - 1
    slot_ids = jnp.arange(TMAX, dtype=jnp.int32)
    picker = ((slot_rank[None, :] == slot_ids[:, None]) & temporal_mask[None, :]).astype(
        jnp.bfloat16
    )
    shaped = [array_in.reshape(tok_len, local_heads, HD) for array_in in (queries, keys, values)]
    lengths = window_lengths[0]
    spatial_out = window_attention(shaped[0], shaped[1], shaped[2], lengths, scaling)
    packed = [compact_heads(array_in, picker)[None] for array_in in shaped]
    query = lax.all_to_all(packed[0], "seq", split_axis=1, concat_axis=0, tiled=True)
    key_rows = lax.all_to_all(packed[1], "seq", split_axis=1, concat_axis=0, tiled=True)
    value_rows = lax.all_to_all(packed[2], "seq", split_axis=1, concat_axis=0, tiled=True)
    sources, width, count, size = query.shape
    groups = sources // FRAMES
    query = query.reshape(FRAMES, groups, width, count, size)
    key_rows = key_rows.reshape(FRAMES, groups, width, count, size)
    value_rows = value_rows.reshape(FRAMES, groups, width, count, size)
    scores = (
        jnp.einsum("fjcnd,gjcnd->jcnfg", query, key_rows, preferred_element_type=jnp.float32)
        * scaling
    )
    weights = softmax_rows(scores).astype(jnp.bfloat16)
    attended = jnp.einsum(
        "jcnfg,gjcnd->fjcnd", weights, value_rows, preferred_element_type=jnp.float32
    ).astype(jnp.bfloat16)
    attended = attended.reshape(sources, width, count, size)
    returned = lax.all_to_all(attended, "seq", split_axis=0, concat_axis=1, tiled=True)
    temporal_out = expand_heads(returned[0], picker)
    mixed = jnp.where(temporal_mask[None, :, None], temporal_out, spatial_out)
    mixed_local = mixed.reshape(tok_len, local_heads * HD)
    mixed_all = lax.all_gather(mixed_local, "head", axis=1, tiled=True)
    summed = jnp.dot(
        mixed_all,
        lax.all_gather(out_weight, "seq", axis=0, tiled=True),
        preferred_element_type=jnp.float32,
    )
    return summed.astype(jnp.bfloat16)


MESH = pl.DeviceIdType.MESH
CHUNKS = 2
VMEM_LIMIT = 62 * 1024 * 1024


def masked_attention(triples, same, scaling):
    scores = [
        lax.dot_general(q, k, (((1,), (1,)), ((), ())), preferred_element_type=jnp.float32)
        for q, k, _ in triples
    ]
    scores = [jnp.where(same, score * scaling, -1e30) for score in scores]
    highest = [jnp.max(score, axis=-1, keepdims=True) for score in scores]
    weights = [jnp.exp(score - top) for score, top in zip(scores, highest)]
    totals = [jnp.sum(weight, axis=-1, keepdims=True) for weight in weights]
    weights = [(weight / total).astype(jnp.bfloat16) for weight, total in zip(weights, totals)]
    return [
        jnp.dot(weight, v, preferred_element_type=jnp.float32).astype(jnp.bfloat16)
        for weight, (_, _, v) in zip(weights, triples)
    ]


def slot_conditions(class_ref, first, local_heads):
    rank = jnp.int32(0)
    taken = []
    for h in range(local_heads):
        flag = (class_ref[first + h] == 1).astype(jnp.int32)
        taken.append([flag * (rank == t).astype(jnp.int32) == 1 for t in range(TMAX)])
        rank = rank + flag
    return taken


def layer_kernel(
    n, groups, class_hbm, len_hbm, q_hbm, k_hbm, v_hbm, w_ref, out_ref,
    class_ref, len_ref, q_ref, k_ref, v_ref,
    packed, landed, spat, spat_in, tsend, temp_in, mixed, w_all, partial,
    up_in, up_out, down_in, down_out,
    load_s, qkv_s, qkv_r, w_s, w_r, w_l, sp_s, sp_r, share_s, share_r, t_s, t_r, tf_s,
    up_s, up_r, down_s, down_r,
):
    pair = n // groups
    seq, head = lax.axis_index("seq"), lax.axis_index("head")
    plane, lane = seq // pair, lax.rem(seq, pair)
    core = lax.rem(head, 2)
    sibling = head + 1 - 2 * core
    across = lax.rem(head + groups // 2, groups)
    tok, columns = q_ref.shape
    local_heads = columns // HD
    width, quarter = tok // n, tok // groups
    chunk = w_ref.shape[1] // CHUNKS
    rows = w_ref.shape[0]
    scaling = 1.0 / math.sqrt(HD)

    def send(src, dst, send_sem, recv_sem, to_seq, to_head):
        return pltpu.make_async_remote_copy(
            src_ref=src, dst_ref=dst, send_sem=send_sem, recv_sem=recv_sem,
            device_id=(to_seq, to_head), device_id_type=MESH,
        )

    loads = [
        pltpu.make_async_copy(src, dst, load_s.at[i])
        for i, (src, dst) in enumerate(
            ((class_hbm, class_ref), (q_hbm, q_ref), (k_hbm, k_ref), (v_hbm, v_ref), (len_hbm, len_ref))
        )
    ]
    for load in loads:
        load.start()
    own_w = pltpu.make_async_copy(w_ref, w_all.at[lane], w_l)
    own_w.start()

    barrier = pltpu.get_barrier_semaphore()

    def greet(to_seq, to_head):
        pl.semaphore_signal(barrier, inc=1, device_id=(to_seq, to_head), device_id_type=MESH)

    for step in range(1, n):
        greet(lax.rem(seq + step, n), head)
    greet(seq, sibling)
    greet(seq, across)

    @pl.when(plane != head)
    def _():
        for peer in range(n):
            greet(jnp.int32(peer), plane)

    for load in loads[:4]:
        load.wait()

    taken = slot_conditions(class_ref, head * local_heads, local_heads)
    for a, ref in enumerate((q_ref, k_ref, v_ref)):
        for t in range(TMAX):
            value = jnp.zeros((tok, HD), jnp.bfloat16)
            for h in range(t, local_heads):
                value = jnp.where(taken[h][t], ref[:, h * HD:(h + 1) * HD], value)
            at = (a * TMAX + t) * HD
            packed[:, :, at:at + HD] = value.reshape(n, width, HD)

    @pl.when(plane == 0)
    def _():
        up_in[...] = jnp.zeros_like(up_in)

    @pl.when(plane == groups - 1)
    def _():
        down_in[...] = jnp.zeros_like(down_in)

    pl.semaphore_wait(barrier, (n - 1) + pair * (groups - 1) + 2)

    qkv = []
    for step in range(1, n):
        peer = lax.rem(seq + step, n)
        copy = send(packed.at[peer], landed.at[seq], qkv_s.at[peer], qkv_r.at[seq], peer, head)
        copy.start()
        qkv.append(copy)
    landed[seq] = packed[seq]

    other = plane * pair + (1 - lane)

    def w_copy(c, owner):
        cols = pl.ds(c * chunk, chunk)
        return send(w_ref.at[:, cols], w_all.at[owner, :, cols], w_s.at[c], w_r.at[c], other, head)

    for c in range(CHUNKS):
        w_copy(c, lane).start()

    loads[4].wait()
    def window_of(axis):
        position = lax.broadcasted_iota(jnp.int32, (tok, tok), axis)
        ids = jnp.zeros((tok, tok), jnp.int32)
        end = jnp.int32(0)
        for i in range(len_ref.shape[1]):
            end = end + len_ref[0, i]
            ids = ids + (position >= end).astype(jnp.int32)
        return ids

    same_window = window_of(0) == window_of(1)
    spans = [slice(h * HD, (h + 1) * HD) for h in range(local_heads)]
    results = masked_attention(
        [(q_ref[:, at], k_ref[:, at], v_ref[:, at]) for at in spans], same_window, scaling
    )
    for at, value in zip(spans, results):
        spat[:, :, at] = value.reshape(groups, quarter, HD)

    at_home = plane == head

    def spatial_copy(step):
        to = lax.rem(head + step, groups)
        return send(
            spat.at[to], spat_in.at[to, plane], sp_s.at[to], sp_r.at[plane], head * pair + lane, to
        )

    for step in range(1, groups):
        spatial_copy(step).start()

    @pl.when(jnp.logical_not(at_home))
    def _():
        spatial_copy(0).start()

    @pl.when(at_home)
    def _():
        spat_in[head, plane] = spat[head]

    for step in range(1, n):
        peer = lax.rem(seq + n - step, n)
        send(landed.at[peer], landed.at[peer], qkv_s.at[peer], qkv_r.at[peer], peer, head).wait_recv()
    row = lax.rem(lax.broadcasted_iota(jnp.int32, (tok, tok), 0), width)
    column = lax.rem(lax.broadcasted_iota(jnp.int32, (tok, tok), 1), width)
    same_position = row == column
    triples = [
        tuple(
            landed[:, :, (a * TMAX + t) * HD:(a * TMAX + t + 1) * HD].reshape(tok, HD)
            for a in range(3)
        )
        for t in range(TMAX)
    ]
    for t, result in enumerate(masked_attention(triples, same_position, scaling)):
        for f in range(n):
            tsend[f % pair, f // pair, :, t * HD:(t + 1) * HD] = result[f * width:(f + 1) * width]

    t_core = lax.rem(seq, 2)
    t_copies = []
    for x in range(pair):
        for y in range(groups // 2):
            to_seq, to_head = head * pair + x, 2 * y + t_core
            mine = (to_seq == seq) & (to_head == head)
            copy = send(tsend.at[x], temp_in.at[seq], t_s.at[x, y], t_r.at[seq], to_seq, to_head)
            t_copies.append((mine, copy))

            @pl.when(jnp.logical_not(mine))
            def _(copy=copy):
                copy.start()

            @pl.when(mine)
            def _(x=x):
                temp_in[seq] = tsend[x]

    def share(which, slot, to_head):
        return send(spat_in.at[which], spat_in.at[which], share_s.at[slot], share_r.at[which], seq, to_head)

    for z in range(groups):
        @pl.when(jnp.logical_not(at_home & (plane == z)))
        def _(z=z):
            send(spat.at[z], spat_in.at[head, z], sp_s.at[z], sp_r.at[z], seq, head).wait_recv()

    share(head, 0, across).start()
    share(head, 1, sibling).start()

    forwards = [share(head, 0, across), share(head, 1, sibling), share(across, 2, sibling)]
    for j in range(n // 2):
        source = 2 * j + core
        here = (source == seq) & (plane == head)
        copy = send(temp_in.at[source], temp_in.at[source], tf_s.at[j], t_r.at[source], seq, sibling)

        @pl.when(jnp.logical_not(here))
        def _(copy=copy):
            copy.wait_recv()

        copy.start()
        forwards.append(copy)
    share(across, 0, across).wait_recv()
    share(across, 2, sibling).start()
    share(sibling, 1, sibling).wait_recv()
    share(lax.rem(sibling + groups // 2, groups), 2, sibling).wait_recv()
    for j in range(n // 2):
        source = 2 * j + 1 - core
        send(temp_in.at[source], temp_in.at[source], tf_s.at[j], t_r.at[source], seq, sibling).wait_recv()

    taken = slot_conditions(class_ref, plane * local_heads, local_heads)
    for z in range(groups):
        for h in range(local_heads):
            value = spat_in[:, z, :, h * HD:(h + 1) * HD].reshape(tok, HD)
            for t in range(min(h + 1, TMAX)):
                slot = temp_in[:, z, :, t * HD:(t + 1) * HD].reshape(tok, HD)
                value = jnp.where(taken[h][t], slot, value)
            mixed[z, :, h * HD:(h + 1) * HD] = value

    own_w.wait()

    def multiply(c):
        w_copy(c, 1 - lane).wait_recv()
        weight = w_all[:, :, c * chunk:(c + 1) * chunk].reshape(pair * rows, chunk)
        result = jnp.dot(
            mixed[...].reshape(groups * tok, columns), weight, preferred_element_type=jnp.float32
        )
        partial[c] = result.reshape(groups, tok, chunk)

    ways = ((1, up_in, up_out, up_s, up_r), (-1, down_in, down_out, down_s, down_r))

    def onward(way, d, c):
        sign, came, goes, s_sem, r_sem = way
        to_seq = seq + sign * pair
        return send(goes.at[d - 1, c], came.at[d - 1, c], s_sem.at[d - 1, c], r_sem.at[d - 1, c], to_seq, head)

    def has_previous(way):
        return plane > 0 if way[0] == 1 else plane < groups - 1

    def reaches(way, d):
        return plane + d < groups if way[0] == 1 else plane >= d

    def arrive(way, d, c):
        @pl.when(has_previous(way))
        def _():
            sign, came, goes, s_sem, r_sem = way
            send(goes.at[d, c], came.at[d, c], s_sem.at[d, c], r_sem.at[d, c], seq, head).wait_recv()

    for c in range(CHUNKS):
        multiply(c)
        for d in range(groups - 1, 0, -1):
            for way in ways:
                @pl.when(reaches(way, d))
                def _(way=way, d=d, c=c):
                    total = partial[c, plane + way[0] * d]
                    if d < groups - 1:
                        arrive(way, d, c)
                        total = total + way[1][d, c].astype(jnp.float32)
                    way[2][d - 1, c] = total.astype(jnp.bfloat16)
                    onward(way, d, c).start()
    for c in range(CHUNKS):
        total = partial[c, plane]
        for way in ways:
            arrive(way, 0, c)
            total = total + way[1][0, c].astype(jnp.float32)
        out_ref[:, c * chunk:(c + 1) * chunk] = total.astype(jnp.bfloat16)

    for copy in qkv:
        copy.wait_send()
    for c in range(CHUNKS):
        w_copy(c, lane).wait_send()
    for step in range(1, groups):
        spatial_copy(step).wait_send()

    @pl.when(jnp.logical_not(at_home))
    def _():
        spatial_copy(0).wait_send()

    for mine, copy in t_copies:
        @pl.when(jnp.logical_not(mine))
        def _(copy=copy):
            copy.wait_send()
    for copy in forwards:
        copy.wait_send()
    for d in range(groups - 1, 0, -1):
        for c in range(CHUNKS):
            for way in ways:
                @pl.when(reaches(way, d))
                def _(way=way, d=d, c=c):
                    onward(way, d, c).wait_send()


def kernel_body(n, groups, queries, keys, values, head_class, window_lengths, out_weight):
    tok, columns = queries.shape
    rows, out_columns = out_weight.shape
    pair, width, quarter = n // groups, tok // n, tok // groups
    chunk = out_columns // CHUNKS
    bf16, dma = jnp.bfloat16, pltpu.SemaphoreType.DMA
    line = (groups - 1, CHUNKS)
    return pl.pallas_call(
        functools.partial(layer_kernel, n, groups),
        out_shape=jax.ShapeDtypeStruct((tok, out_columns), bf16),
        in_specs=[pl.BlockSpec(memory_space=pl.ANY)] * 6,
        out_specs=pl.BlockSpec(memory_space=pltpu.VMEM),
        scratch_shapes=[
            pltpu.SMEM(head_class.shape, jnp.int32),
            pltpu.SMEM(window_lengths.shape, jnp.int32),
            pltpu.VMEM((tok, columns), bf16),
            pltpu.VMEM((tok, columns), bf16),
            pltpu.VMEM((tok, columns), bf16),
            pltpu.VMEM((n, width, 3 * TMAX * HD), bf16),
            pltpu.VMEM((n, width, 3 * TMAX * HD), bf16),
            pltpu.VMEM((groups, quarter, columns), bf16),
            pltpu.VMEM((groups, groups, quarter, columns), bf16),
            pltpu.VMEM((pair, groups, width, TMAX * HD), bf16),
            pltpu.VMEM((n, groups, width, TMAX * HD), bf16),
            pltpu.VMEM((groups, tok, columns), bf16),
            pltpu.VMEM((pair, rows, out_columns), bf16),
            pltpu.VMEM((CHUNKS, groups, tok, chunk), jnp.float32),
            pltpu.VMEM(line + (tok, chunk), bf16),
            pltpu.VMEM(line + (tok, chunk), bf16),
            pltpu.VMEM(line + (tok, chunk), bf16),
            pltpu.VMEM(line + (tok, chunk), bf16),
            dma((5,)), dma((n,)), dma((n,)),
            dma((CHUNKS,)), dma((CHUNKS,)), dma,
            dma((groups,)), dma((groups,)), dma((3,)), dma((groups,)),
            dma((pair, groups // 2)), dma((n,)), dma((n // 2,)),
            dma(line), dma(line), dma(line), dma(line),
        ],
        compiler_params=pltpu.CompilerParams(
            collective_id=0, has_side_effects=True, vmem_limit_bytes=VMEM_LIMIT
        ),
        cost_estimate=pl.CostEstimate(
            flops=2 * groups * tok * columns * out_columns,
            bytes_accessed=4 * rows * out_columns,
            transcendentals=local_count(columns) * tok * tok,
        ),
    )(head_class, window_lengths, queries, keys, values, out_weight)


def local_count(columns):
    return columns // HD + TMAX


def solution(mesh):
    n, groups = mesh.shape["seq"], mesh.shape["head"]

    def body(queries, keys, values, head_class, window_lengths, out_weight):
        tok, rows = queries.shape[0], out_weight.shape[0]
        if n == FRAMES and n == 2 * groups and rows > tok:
            return kernel_body(
                n, groups, queries, keys, values, head_class, window_lengths, out_weight
            )
        return gather_body(queries, keys, values, head_class, window_lengths, out_weight)

    placed = (
        P("seq", "head"),
        P("seq", "head"),
        P("seq", "head"),
        P(),
        P("seq", None),
        P("seq", "head"),
    )
    return jax.shard_map(
        body, mesh=mesh, in_specs=placed, out_specs=P("seq", "head"), check_vma=False
    )
```

```python
import functools
import math

import jax
import jax.numpy as jnp
from jax import lax
from jax.experimental import pallas as pl
from jax.experimental.pallas import tpu as pltpu
from jax.sharding import PartitionSpec as P

HD = 128
TMAX = 3
FRAMES = 8


def softmax_rows(scores):
    highest = jnp.max(scores, axis=-1, keepdims=True)
    weights = jnp.exp(scores - highest)
    return weights / jnp.sum(weights, axis=-1, keepdims=True)


def compact_heads(source, picker):
    return jnp.einsum("shd,th->std", source, picker, preferred_element_type=jnp.float32).astype(
        jnp.bfloat16
    )


def expand_heads(source, picker):
    return jnp.einsum("std,th->shd", source, picker, preferred_element_type=jnp.float32).astype(
        jnp.bfloat16
    )


def window_attention(query, key_rows, value_rows, lengths, scaling):
    ends = jnp.cumsum(lengths)
    positions = jnp.arange(query.shape[0], dtype=jnp.int32)
    window_ids = jnp.sum((positions[:, None] >= ends[None, :]).astype(jnp.int32), axis=1)
    same_window = window_ids[:, None] == window_ids[None, :]
    scores = (
        jnp.einsum("shd,thd->hst", query, key_rows, preferred_element_type=jnp.float32) * scaling
    )
    scores = jnp.where(same_window[None], scores, -1e30)
    weights = softmax_rows(scores).astype(jnp.bfloat16)
    return jnp.einsum(
        "hst,thd->shd", weights, value_rows, preferred_element_type=jnp.float32
    ).astype(jnp.bfloat16)


def gather_body(queries, keys, values, head_class, window_lengths, out_weight):
    tok_len, columns = queries.shape
    local_heads = columns // HD
    scaling = 1.0 / math.sqrt(HD)
    head_group = lax.axis_index("head")
    classes = lax.dynamic_slice_in_dim(head_class, head_group * local_heads, local_heads)
    temporal_mask = classes == 1
    slot_rank = jnp.cumsum(temporal_mask.astype(jnp.int32)) - 1
    slot_ids = jnp.arange(TMAX, dtype=jnp.int32)
    picker = ((slot_rank[None, :] == slot_ids[:, None]) & temporal_mask[None, :]).astype(
        jnp.bfloat16
    )
    shaped = [array_in.reshape(tok_len, local_heads, HD) for array_in in (queries, keys, values)]
    lengths = window_lengths[0]
    spatial_out = window_attention(shaped[0], shaped[1], shaped[2], lengths, scaling)
    packed = [compact_heads(array_in, picker)[None] for array_in in shaped]
    query = lax.all_to_all(packed[0], "seq", split_axis=1, concat_axis=0, tiled=True)
    key_rows = lax.all_to_all(packed[1], "seq", split_axis=1, concat_axis=0, tiled=True)
    value_rows = lax.all_to_all(packed[2], "seq", split_axis=1, concat_axis=0, tiled=True)
    sources, width, count, size = query.shape
    groups = sources // FRAMES
    query = query.reshape(FRAMES, groups, width, count, size)
    key_rows = key_rows.reshape(FRAMES, groups, width, count, size)
    value_rows = value_rows.reshape(FRAMES, groups, width, count, size)
    scores = (
        jnp.einsum("fjcnd,gjcnd->jcnfg", query, key_rows, preferred_element_type=jnp.float32)
        * scaling
    )
    weights = softmax_rows(scores).astype(jnp.bfloat16)
    attended = jnp.einsum(
        "jcnfg,gjcnd->fjcnd", weights, value_rows, preferred_element_type=jnp.float32
    ).astype(jnp.bfloat16)
    attended = attended.reshape(sources, width, count, size)
    returned = lax.all_to_all(attended, "seq", split_axis=0, concat_axis=1, tiled=True)
    temporal_out = expand_heads(returned[0], picker)
    mixed = jnp.where(temporal_mask[None, :, None], temporal_out, spatial_out)
    mixed_local = mixed.reshape(tok_len, local_heads * HD)
    mixed_all = lax.all_gather(mixed_local, "head", axis=1, tiled=True)
    summed = jnp.dot(
        mixed_all,
        lax.all_gather(out_weight, "seq", axis=0, tiled=True),
        preferred_element_type=jnp.float32,
    )
    return summed.astype(jnp.bfloat16)


MESH = pl.DeviceIdType.MESH
CHUNKS = 2
VMEM_LIMIT = 62 * 1024 * 1024


def masked_attention(triples, same, scaling):
    scores = [
        lax.dot_general(q, k, (((1,), (1,)), ((), ())), preferred_element_type=jnp.float32)
        for q, k, _ in triples
    ]
    scores = [jnp.where(same, score * scaling, -1e30) for score in scores]
    highest = [jnp.max(score, axis=-1, keepdims=True) for score in scores]
    weights = [jnp.exp(score - top) for score, top in zip(scores, highest)]
    totals = [jnp.sum(weight, axis=-1, keepdims=True) for weight in weights]
    weights = [(weight / total).astype(jnp.bfloat16) for weight, total in zip(weights, totals)]
    return [
        jnp.dot(weight, v, preferred_element_type=jnp.float32).astype(jnp.bfloat16)
        for weight, (_, _, v) in zip(weights, triples)
    ]


def slot_conditions(class_ref, first, local_heads):
    rank = jnp.int32(0)
    taken = []
    for h in range(local_heads):
        flag = (class_ref[first + h] == 1).astype(jnp.int32)
        taken.append([flag * (rank == t).astype(jnp.int32) == 1 for t in range(TMAX)])
        rank = rank + flag
    return taken


def layer_kernel(
    n, groups, class_hbm, len_hbm, q_hbm, k_hbm, v_hbm, w_ref, out_ref,
    class_ref, len_ref, q_ref, k_ref, v_ref,
    packed, landed, spat, spat_in, tsend, temp_in, mixed, w_all, partial,
    up_in, up_out, down_in, down_out,
    load_s, qkv_s, qkv_r, w_s, w_r, w_l, sp_s, sp_r, sp_l, spf_s, t_s, t_r, t_l, tf_s,
    up_s, up_r, down_s, down_r,
):
    pair = n // groups
    seq, head = lax.axis_index("seq"), lax.axis_index("head")
    plane, lane = seq // pair, lax.rem(seq, pair)
    core = lax.rem(head, 2)
    sibling = head + 1 - 2 * core
    tok, columns = q_ref.shape
    local_heads = columns // HD
    width = tok // n
    chunk = w_ref.shape[1] // CHUNKS
    rows = w_ref.shape[0]
    scaling = 1.0 / math.sqrt(HD)

    def send(src, dst, send_sem, recv_sem, to_seq, to_head):
        return pltpu.make_async_remote_copy(
            src_ref=src, dst_ref=dst, send_sem=send_sem, recv_sem=recv_sem,
            device_id=(to_seq, to_head), device_id_type=MESH,
        )

    loads = [
        pltpu.make_async_copy(src, dst, load_s.at[i])
        for i, (src, dst) in enumerate(
            ((class_hbm, class_ref), (q_hbm, q_ref), (k_hbm, k_ref), (v_hbm, v_ref), (len_hbm, len_ref))
        )
    ]
    for load in loads:
        load.start()
    own_w = pltpu.make_async_copy(w_ref, w_all.at[lane], w_l)
    own_w.start()

    barrier = pltpu.get_barrier_semaphore()

    def greet(to_seq, to_head):
        pl.semaphore_signal(barrier, inc=1, device_id=(to_seq, to_head), device_id_type=MESH)

    for step in range(1, n):
        greet(lax.rem(seq + step, n), head)
    greet(seq, sibling)

    @pl.when(plane != head)
    def _():
        for peer in range(n):
            greet(jnp.int32(peer), plane)

    for load in loads[:4]:
        load.wait()

    taken = slot_conditions(class_ref, head * local_heads, local_heads)
    for a, ref in enumerate((q_ref, k_ref, v_ref)):
        for t in range(TMAX):
            value = jnp.zeros((tok, HD), jnp.bfloat16)
            for h in range(t, local_heads):
                value = jnp.where(taken[h][t], ref[:, h * HD:(h + 1) * HD], value)
            at = (a * TMAX + t) * HD
            packed[:, :, at:at + HD] = value.reshape(n, width, HD)

    @pl.when(plane == 0)
    def _():
        up_in[...] = jnp.zeros_like(up_in)

    @pl.when(plane == groups - 1)
    def _():
        down_in[...] = jnp.zeros_like(down_in)

    pl.semaphore_wait(barrier, (n - 1) + pair * (groups - 1) + 1)

    qkv = []
    for step in range(1, n):
        peer = lax.rem(seq + step, n)
        copy = send(packed.at[peer], landed.at[seq], qkv_s.at[peer], qkv_r.at[seq], peer, head)
        copy.start()
        qkv.append(copy)
    landed[seq] = packed[seq]

    other = plane * pair + (1 - lane)

    def w_copy(c, owner):
        cols = pl.ds(c * chunk, chunk)
        return send(w_ref.at[:, cols], w_all.at[owner, :, cols], w_s.at[c], w_r.at[c], other, head)

    @pl.when(core == 0)
    def _():
        for c in range(CHUNKS):
            w_copy(c, lane).start()

    loads[4].wait()
    def window_of(axis):
        position = lax.broadcasted_iota(jnp.int32, (tok, tok), axis)
        ids = jnp.zeros((tok, tok), jnp.int32)
        end = jnp.int32(0)
        for i in range(len_ref.shape[1]):
            end = end + len_ref[0, i]
            ids = ids + (position >= end).astype(jnp.int32)
        return ids

    same_window = window_of(0) == window_of(1)
    spans = [slice(h * HD, (h + 1) * HD) for h in range(local_heads)]
    results = masked_attention(
        [(q_ref[:, at], k_ref[:, at], v_ref[:, at]) for at in spans], same_window, scaling
    )
    for at, value in zip(spans, results):
        spat[:, at] = value

    sp_core = lax.rem(plane, 2)
    sp_copies = []
    for y in range(groups // 2):
        to_seq, to_head = head * pair + lane, 2 * y + sp_core
        mine = (to_seq == seq) & (to_head == head)
        copy = send(spat, spat_in.at[plane], sp_s.at[y], sp_r.at[plane], to_seq, to_head)
        sp_copies.append((mine, copy))

        @pl.when(jnp.logical_not(mine))
        def _(copy=copy):
            copy.start()

        @pl.when(mine)
        def _():
            spat_in[plane] = spat[...]

    for step in range(1, n):
        peer = lax.rem(seq + n - step, n)
        send(landed.at[peer], landed.at[peer], qkv_s.at[peer], qkv_r.at[peer], peer, head).wait_recv()
    row = lax.rem(lax.broadcasted_iota(jnp.int32, (tok, tok), 0), width)
    column = lax.rem(lax.broadcasted_iota(jnp.int32, (tok, tok), 1), width)
    same_position = row == column
    triples = [
        tuple(
            landed[:, :, (a * TMAX + t) * HD:(a * TMAX + t + 1) * HD].reshape(tok, HD)
            for a in range(3)
        )
        for t in range(TMAX)
    ]
    for t, result in enumerate(masked_attention(triples, same_position, scaling)):
        for f in range(n):
            tsend[f % pair, f // pair, :, t * HD:(t + 1) * HD] = result[f * width:(f + 1) * width]

    t_core = lax.rem(seq, 2)
    t_copies = []
    for x in range(pair):
        for y in range(groups // 2):
            to_seq, to_head = head * pair + x, 2 * y + t_core
            mine = (to_seq == seq) & (to_head == head)
            copy = send(tsend.at[x], temp_in.at[seq], t_s.at[x, y], t_r.at[seq], to_seq, to_head)
            t_copies.append((mine, copy))

            @pl.when(jnp.logical_not(mine))
            def _(copy=copy):
                copy.start()

            @pl.when(mine)
            def _(x=x):
                temp_in[seq] = tsend[x]

    @pl.when(core == 1)
    def _():
        w_copy(0, lane).start()

    forwards = []
    for j in range(groups // 2):
        source = 2 * j + core
        here = (source == plane) & (plane == head)
        copy = send(spat_in.at[source], spat_in.at[source], spf_s.at[j], sp_r.at[source], seq, sibling)

        @pl.when(jnp.logical_not(here))
        def _(copy=copy):
            copy.wait_recv()

        copy.start()
        forwards.append(copy)
    for j in range(n // 2):
        source = 2 * j + core
        here = (source == seq) & (plane == head)
        copy = send(temp_in.at[source], temp_in.at[source], tf_s.at[j], t_r.at[source], seq, sibling)

        @pl.when(jnp.logical_not(here))
        def _(copy=copy):
            copy.wait_recv()

        copy.start()
        forwards.append(copy)

    @pl.when(core == 1)
    def _():
        for c in range(1, CHUNKS):
            w_copy(c, lane).start()

    for j in range(groups // 2):
        source = 2 * j + 1 - core
        send(spat_in.at[source], spat_in.at[source], spf_s.at[j], sp_r.at[source], seq, sibling).wait_recv()
    for j in range(n // 2):
        source = 2 * j + 1 - core
        send(temp_in.at[source], temp_in.at[source], tf_s.at[j], t_r.at[source], seq, sibling).wait_recv()

    taken = slot_conditions(class_ref, plane * local_heads, local_heads)
    for z in range(groups):
        for h in range(local_heads):
            value = spat_in[z, :, h * HD:(h + 1) * HD]
            for t in range(min(h + 1, TMAX)):
                slot = temp_in[:, z, :, t * HD:(t + 1) * HD].reshape(tok, HD)
                value = jnp.where(taken[h][t], slot, value)
            mixed[z, :, h * HD:(h + 1) * HD] = value

    own_w.wait()

    def multiply(c):
        w_copy(c, 1 - lane).wait_recv()
        weight = w_all[:, :, c * chunk:(c + 1) * chunk].reshape(pair * rows, chunk)
        result = jnp.dot(
            mixed[...].reshape(groups * tok, columns), weight, preferred_element_type=jnp.float32
        )
        partial[c] = result.reshape(groups, tok, chunk)

    ways = ((1, up_in, up_out, up_s, up_r), (-1, down_in, down_out, down_s, down_r))

    def onward(way, d, c):
        sign, came, goes, s_sem, r_sem = way
        to_seq = seq + sign * pair
        return send(goes.at[d - 1, c], came.at[d - 1, c], s_sem.at[d - 1, c], r_sem.at[d - 1, c], to_seq, head)

    def has_previous(way):
        return plane > 0 if way[0] == 1 else plane < groups - 1

    def reaches(way, d):
        return plane + d < groups if way[0] == 1 else plane >= d

    def arrive(way, d, c):
        @pl.when(has_previous(way))
        def _():
            sign, came, goes, s_sem, r_sem = way
            send(goes.at[d, c], came.at[d, c], s_sem.at[d, c], r_sem.at[d, c], seq, head).wait_recv()

    for c in range(CHUNKS):
        multiply(c)
        for d in range(groups - 1, 0, -1):
            for way in ways:
                @pl.when(reaches(way, d))
                def _(way=way, d=d, c=c):
                    total = partial[c, plane + way[0] * d]
                    if d < groups - 1:
                        arrive(way, d, c)
                        total = total + way[1][d, c].astype(jnp.float32)
                    way[2][d - 1, c] = total.astype(jnp.bfloat16)
                    onward(way, d, c).start()
    for c in range(CHUNKS):
        total = partial[c, plane]
        for way in ways:
            arrive(way, 0, c)
            total = total + way[1][0, c].astype(jnp.float32)
        out_ref[:, c * chunk:(c + 1) * chunk] = total.astype(jnp.bfloat16)

    for copy in qkv:
        copy.wait_send()
    for c in range(CHUNKS):
        w_copy(c, lane).wait_send()
    for mine, copy in sp_copies + t_copies:
        @pl.when(jnp.logical_not(mine))
        def _(copy=copy):
            copy.wait_send()
    for copy in forwards:
        copy.wait_send()
    for d in range(groups - 1, 0, -1):
        for c in range(CHUNKS):
            for way in ways:
                @pl.when(reaches(way, d))
                def _(way=way, d=d, c=c):
                    onward(way, d, c).wait_send()


def kernel_body(n, groups, queries, keys, values, head_class, window_lengths, out_weight):
    tok, columns = queries.shape
    rows, out_columns = out_weight.shape
    pair, width = n // groups, tok // n
    chunk = out_columns // CHUNKS
    bf16, dma = jnp.bfloat16, pltpu.SemaphoreType.DMA
    line = (groups - 1, CHUNKS)
    return pl.pallas_call(
        functools.partial(layer_kernel, n, groups),
        out_shape=jax.ShapeDtypeStruct((tok, out_columns), bf16),
        in_specs=[pl.BlockSpec(memory_space=pl.ANY)] * 6,
        out_specs=pl.BlockSpec(memory_space=pltpu.VMEM),
        scratch_shapes=[
            pltpu.SMEM(head_class.shape, jnp.int32),
            pltpu.SMEM(window_lengths.shape, jnp.int32),
            pltpu.VMEM((tok, columns), bf16),
            pltpu.VMEM((tok, columns), bf16),
            pltpu.VMEM((tok, columns), bf16),
            pltpu.VMEM((n, width, 3 * TMAX * HD), bf16),
            pltpu.VMEM((n, width, 3 * TMAX * HD), bf16),
            pltpu.VMEM((tok, columns), bf16),
            pltpu.VMEM((groups, tok, columns), bf16),
            pltpu.VMEM((pair, groups, width, TMAX * HD), bf16),
            pltpu.VMEM((n, groups, width, TMAX * HD), bf16),
            pltpu.VMEM((groups, tok, columns), bf16),
            pltpu.VMEM((pair, rows, out_columns), bf16),
            pltpu.VMEM((CHUNKS, groups, tok, chunk), jnp.float32),
            pltpu.VMEM(line + (tok, chunk), bf16),
            pltpu.VMEM(line + (tok, chunk), bf16),
            pltpu.VMEM(line + (tok, chunk), bf16),
            pltpu.VMEM(line + (tok, chunk), bf16),
            dma((5,)), dma((n,)), dma((n,)),
            dma((CHUNKS,)), dma((CHUNKS,)), dma,
            dma((groups // 2,)), dma((groups,)), dma, dma((groups // 2,)),
            dma((pair, groups // 2)), dma((n,)), dma, dma((n // 2,)),
            dma(line), dma(line), dma(line), dma(line),
        ],
        compiler_params=pltpu.CompilerParams(
            collective_id=0, has_side_effects=True, vmem_limit_bytes=VMEM_LIMIT
        ),
        cost_estimate=pl.CostEstimate(
            flops=2 * groups * tok * columns * out_columns,
            bytes_accessed=4 * rows * out_columns,
            transcendentals=local_count(columns) * tok * tok,
        ),
    )(head_class, window_lengths, queries, keys, values, out_weight)


def local_count(columns):
    return columns // HD + TMAX


def solution(mesh):
    n, groups = mesh.shape["seq"], mesh.shape["head"]

    def body(queries, keys, values, head_class, window_lengths, out_weight):
        tok, rows = queries.shape[0], out_weight.shape[0]
        if n == FRAMES and n == 2 * groups and rows > tok:
            return kernel_body(
                n, groups, queries, keys, values, head_class, window_lengths, out_weight
            )
        return gather_body(queries, keys, values, head_class, window_lengths, out_weight)

    placed = (
        P("seq", "head"),
        P("seq", "head"),
        P("seq", "head"),
        P(),
        P("seq", None),
        P("seq", "head"),
    )
    return jax.shard_map(
        body, mesh=mesh, in_specs=placed, out_specs=P("seq", "head"), check_vma=False
    )
```

```python
import functools
import math

import jax
import jax.numpy as jnp
from jax import lax
from jax.experimental import pallas as pl
from jax.experimental.pallas import tpu as pltpu
from jax.sharding import PartitionSpec as P

HD = 128
TMAX = 3
FRAMES = 8


def softmax_rows(scores):
    highest = jnp.max(scores, axis=-1, keepdims=True)
    weights = jnp.exp(scores - highest)
    return weights / jnp.sum(weights, axis=-1, keepdims=True)


def compact_heads(source, picker):
    return jnp.einsum("shd,th->std", source, picker, preferred_element_type=jnp.float32).astype(
        jnp.bfloat16
    )


def expand_heads(source, picker):
    return jnp.einsum("std,th->shd", source, picker, preferred_element_type=jnp.float32).astype(
        jnp.bfloat16
    )


def window_attention(query, key_rows, value_rows, lengths, scaling):
    ends = jnp.cumsum(lengths)
    positions = jnp.arange(query.shape[0], dtype=jnp.int32)
    window_ids = jnp.sum((positions[:, None] >= ends[None, :]).astype(jnp.int32), axis=1)
    same_window = window_ids[:, None] == window_ids[None, :]
    scores = (
        jnp.einsum("shd,thd->hst", query, key_rows, preferred_element_type=jnp.float32) * scaling
    )
    scores = jnp.where(same_window[None], scores, -1e30)
    weights = softmax_rows(scores).astype(jnp.bfloat16)
    return jnp.einsum(
        "hst,thd->shd", weights, value_rows, preferred_element_type=jnp.float32
    ).astype(jnp.bfloat16)


def gather_body(queries, keys, values, head_class, window_lengths, out_weight):
    tok_len, columns = queries.shape
    local_heads = columns // HD
    scaling = 1.0 / math.sqrt(HD)
    head_group = lax.axis_index("head")
    classes = lax.dynamic_slice_in_dim(head_class, head_group * local_heads, local_heads)
    temporal_mask = classes == 1
    slot_rank = jnp.cumsum(temporal_mask.astype(jnp.int32)) - 1
    slot_ids = jnp.arange(TMAX, dtype=jnp.int32)
    picker = ((slot_rank[None, :] == slot_ids[:, None]) & temporal_mask[None, :]).astype(
        jnp.bfloat16
    )
    shaped = [array_in.reshape(tok_len, local_heads, HD) for array_in in (queries, keys, values)]
    lengths = window_lengths[0]
    spatial_out = window_attention(shaped[0], shaped[1], shaped[2], lengths, scaling)
    packed = [compact_heads(array_in, picker)[None] for array_in in shaped]
    query = lax.all_to_all(packed[0], "seq", split_axis=1, concat_axis=0, tiled=True)
    key_rows = lax.all_to_all(packed[1], "seq", split_axis=1, concat_axis=0, tiled=True)
    value_rows = lax.all_to_all(packed[2], "seq", split_axis=1, concat_axis=0, tiled=True)
    sources, width, count, size = query.shape
    groups = sources // FRAMES
    query = query.reshape(FRAMES, groups, width, count, size)
    key_rows = key_rows.reshape(FRAMES, groups, width, count, size)
    value_rows = value_rows.reshape(FRAMES, groups, width, count, size)
    scores = (
        jnp.einsum("fjcnd,gjcnd->jcnfg", query, key_rows, preferred_element_type=jnp.float32)
        * scaling
    )
    weights = softmax_rows(scores).astype(jnp.bfloat16)
    attended = jnp.einsum(
        "jcnfg,gjcnd->fjcnd", weights, value_rows, preferred_element_type=jnp.float32
    ).astype(jnp.bfloat16)
    attended = attended.reshape(sources, width, count, size)
    returned = lax.all_to_all(attended, "seq", split_axis=0, concat_axis=1, tiled=True)
    temporal_out = expand_heads(returned[0], picker)
    mixed = jnp.where(temporal_mask[None, :, None], temporal_out, spatial_out)
    mixed_local = mixed.reshape(tok_len, local_heads * HD)
    mixed_all = lax.all_gather(mixed_local, "head", axis=1, tiled=True)
    summed = jnp.dot(
        mixed_all,
        lax.all_gather(out_weight, "seq", axis=0, tiled=True),
        preferred_element_type=jnp.float32,
    )
    return summed.astype(jnp.bfloat16)


MESH = pl.DeviceIdType.MESH
CHUNKS = 2
VMEM_LIMIT = 62 * 1024 * 1024


def masked_attention(triples, same, scaling):
    scores = [
        lax.dot_general(q, k, (((1,), (1,)), ((), ())), preferred_element_type=jnp.float32)
        for q, k, _ in triples
    ]
    scores = [jnp.where(same, score * scaling, -1e30) for score in scores]
    highest = [jnp.max(score, axis=-1, keepdims=True) for score in scores]
    weights = [jnp.exp(score - top) for score, top in zip(scores, highest)]
    totals = [jnp.sum(weight, axis=-1, keepdims=True) for weight in weights]
    weights = [(weight / total).astype(jnp.bfloat16) for weight, total in zip(weights, totals)]
    return [
        jnp.dot(weight, v, preferred_element_type=jnp.float32).astype(jnp.bfloat16)
        for weight, (_, _, v) in zip(weights, triples)
    ]


def slot_conditions(class_ref, first, local_heads):
    rank = jnp.int32(0)
    taken = []
    for h in range(local_heads):
        flag = (class_ref[first + h] == 1).astype(jnp.int32)
        taken.append([flag * (rank == t).astype(jnp.int32) == 1 for t in range(TMAX)])
        rank = rank + flag
    return taken


def layer_kernel(
    n, groups, class_hbm, len_hbm, q_hbm, k_hbm, v_hbm, w_ref, out_ref,
    class_ref, len_ref, q_ref, k_ref, v_ref,
    packed, landed, spat, spat_in, tsend, temp_in, mixed, w_all, partial,
    up_in, up_out, down_in, down_out,
    load_s, qkv_s, qkv_r, w_s, w_r, w_l, sp_s, sp_r, share_s, share_r, t_s, t_r, tf_s,
    up_s, up_r, down_s, down_r,
):
    pair = n // groups
    seq, head = lax.axis_index("seq"), lax.axis_index("head")
    plane, lane = seq // pair, lax.rem(seq, pair)
    core = lax.rem(head, 2)
    sibling = head + 1 - 2 * core
    across = lax.rem(head + groups // 2, groups)
    tok, columns = q_ref.shape
    local_heads = columns // HD
    width, quarter = tok // n, tok // groups
    chunk = w_ref.shape[1] // CHUNKS
    rows = w_ref.shape[0]
    scaling = 1.0 / math.sqrt(HD)

    def send(src, dst, send_sem, recv_sem, to_seq, to_head):
        return pltpu.make_async_remote_copy(
            src_ref=src, dst_ref=dst, send_sem=send_sem, recv_sem=recv_sem,
            device_id=(to_seq, to_head), device_id_type=MESH,
        )

    loads = [
        pltpu.make_async_copy(src, dst, load_s.at[i])
        for i, (src, dst) in enumerate(
            ((class_hbm, class_ref), (q_hbm, q_ref), (k_hbm, k_ref), (v_hbm, v_ref), (len_hbm, len_ref))
        )
    ]
    for load in loads:
        load.start()
    own_w = pltpu.make_async_copy(w_ref, w_all.at[lane], w_l)
    own_w.start()

    barrier = pltpu.get_barrier_semaphore()

    def greet(to_seq, to_head):
        pl.semaphore_signal(barrier, inc=1, device_id=(to_seq, to_head), device_id_type=MESH)

    for step in range(1, n):
        greet(lax.rem(seq + step, n), head)
    greet(seq, sibling)
    greet(seq, across)

    @pl.when(plane != head)
    def _():
        for peer in range(n):
            greet(jnp.int32(peer), plane)

    for load in loads[:4]:
        load.wait()

    taken = slot_conditions(class_ref, head * local_heads, local_heads)
    for a, ref in enumerate((q_ref, k_ref, v_ref)):
        for t in range(TMAX):
            value = jnp.zeros((tok, HD), jnp.bfloat16)
            for h in range(t, local_heads):
                value = jnp.where(taken[h][t], ref[:, h * HD:(h + 1) * HD], value)
            at = (a * TMAX + t) * HD
            packed[:, :, at:at + HD] = value.reshape(n, width, HD)

    @pl.when(plane == 0)
    def _():
        up_in[...] = jnp.zeros_like(up_in)

    @pl.when(plane == groups - 1)
    def _():
        down_in[...] = jnp.zeros_like(down_in)

    pl.semaphore_wait(barrier, (n - 1) + pair * (groups - 1) + 2)

    qkv = []
    for step in range(1, n):
        peer = lax.rem(seq + step, n)
        copy = send(packed.at[peer], landed.at[seq], qkv_s.at[peer], qkv_r.at[seq], peer, head)
        copy.start()
        qkv.append(copy)
    landed[seq] = packed[seq]

    other = plane * pair + (1 - lane)

    def w_copy(owner):
        return send(w_ref, w_all.at[owner], w_s, w_r, other, head)

    w_copy(lane).start()

    loads[4].wait()
    def window_of(axis):
        position = lax.broadcasted_iota(jnp.int32, (tok, tok), axis)
        ids = jnp.zeros((tok, tok), jnp.int32)
        end = jnp.int32(0)
        for i in range(len_ref.shape[1]):
            end = end + len_ref[0, i]
            ids = ids + (position >= end).astype(jnp.int32)
        return ids

    same_window = window_of(0) == window_of(1)
    spans = [slice(h * HD, (h + 1) * HD) for h in range(local_heads)]
    results = masked_attention(
        [(q_ref[:, at], k_ref[:, at], v_ref[:, at]) for at in spans], same_window, scaling
    )
    for at, value in zip(spans, results):
        spat[:, :, at] = value.reshape(groups, quarter, HD)

    at_home = plane == head

    def spatial_copy(step):
        to = lax.rem(head + step, groups)
        return send(
            spat.at[to], spat_in.at[to, plane], sp_s.at[to], sp_r.at[plane], head * pair + lane, to
        )

    for step in range(1, groups):
        spatial_copy(step).start()

    @pl.when(jnp.logical_not(at_home))
    def _():
        spatial_copy(0).start()

    @pl.when(at_home)
    def _():
        spat_in[head, plane] = spat[head]

    for step in range(1, n):
        peer = lax.rem(seq + n - step, n)
        send(landed.at[peer], landed.at[peer], qkv_s.at[peer], qkv_r.at[peer], peer, head).wait_recv()
    row = lax.rem(lax.broadcasted_iota(jnp.int32, (tok, tok), 0), width)
    column = lax.rem(lax.broadcasted_iota(jnp.int32, (tok, tok), 1), width)
    same_position = row == column
    triples = [
        tuple(
            landed[:, :, (a * TMAX + t) * HD:(a * TMAX + t + 1) * HD].reshape(tok, HD)
            for a in range(3)
        )
        for t in range(TMAX)
    ]
    for t, result in enumerate(masked_attention(triples, same_position, scaling)):
        for f in range(n):
            tsend[f % pair, f // pair, :, t * HD:(t + 1) * HD] = result[f * width:(f + 1) * width]

    t_core = lax.rem(seq, 2)
    t_copies = []
    for x in range(pair):
        for y in range(groups // 2):
            to_seq, to_head = head * pair + x, 2 * y + t_core
            mine = (to_seq == seq) & (to_head == head)
            copy = send(tsend.at[x], temp_in.at[seq], t_s.at[x, y], t_r.at[seq], to_seq, to_head)
            t_copies.append((mine, copy))

            @pl.when(jnp.logical_not(mine))
            def _(copy=copy):
                copy.start()

            @pl.when(mine)
            def _(x=x):
                temp_in[seq] = tsend[x]

    def share(which, slot, to_head):
        return send(spat_in.at[which], spat_in.at[which], share_s.at[slot], share_r.at[which], seq, to_head)

    for z in range(groups):
        @pl.when(jnp.logical_not(at_home & (plane == z)))
        def _(z=z):
            send(spat.at[z], spat_in.at[head, z], sp_s.at[z], sp_r.at[z], seq, head).wait_recv()

    share(head, 0, across).start()
    share(head, 1, sibling).start()

    forwards = [share(head, 0, across), share(head, 1, sibling), share(across, 2, sibling)]
    for j in range(n // 2):
        source = 2 * j + core
        here = (source == seq) & (plane == head)
        copy = send(temp_in.at[source], temp_in.at[source], tf_s.at[j], t_r.at[source], seq, sibling)

        @pl.when(jnp.logical_not(here))
        def _(copy=copy):
            copy.wait_recv()

        copy.start()
        forwards.append(copy)
    share(across, 0, across).wait_recv()
    share(across, 2, sibling).start()
    share(sibling, 1, sibling).wait_recv()
    share(lax.rem(sibling + groups // 2, groups), 2, sibling).wait_recv()
    for j in range(n // 2):
        source = 2 * j + 1 - core
        send(temp_in.at[source], temp_in.at[source], tf_s.at[j], t_r.at[source], seq, sibling).wait_recv()

    taken = slot_conditions(class_ref, plane * local_heads, local_heads)
    for z in range(groups):
        for h in range(local_heads):
            value = spat_in[:, z, :, h * HD:(h + 1) * HD].reshape(tok, HD)
            for t in range(min(h + 1, TMAX)):
                slot = temp_in[:, z, :, t * HD:(t + 1) * HD].reshape(tok, HD)
                value = jnp.where(taken[h][t], slot, value)
            mixed[z, :, h * HD:(h + 1) * HD] = value

    own_w.wait()
    w_copy(1 - lane).wait_recv()

    def multiply(c):
        weight = w_all[:, :, c * chunk:(c + 1) * chunk].reshape(pair * rows, chunk)
        result = jnp.dot(
            mixed[...].reshape(groups * tok, columns), weight, preferred_element_type=jnp.float32
        )
        partial[c] = result.reshape(groups, tok, chunk)

    ways = ((1, up_in, up_out, up_s, up_r), (-1, down_in, down_out, down_s, down_r))

    def onward(way, d, c):
        sign, came, goes, s_sem, r_sem = way
        to_seq = seq + sign * pair
        return send(goes.at[d - 1, c], came.at[d - 1, c], s_sem.at[d - 1, c], r_sem.at[d - 1, c], to_seq, head)

    def has_previous(way):
        return plane > 0 if way[0] == 1 else plane < groups - 1

    def reaches(way, d):
        return plane + d < groups if way[0] == 1 else plane >= d

    def arrive(way, d, c):
        @pl.when(has_previous(way))
        def _():
            sign, came, goes, s_sem, r_sem = way
            send(goes.at[d, c], came.at[d, c], s_sem.at[d, c], r_sem.at[d, c], seq, head).wait_recv()

    for d in range(groups - 1, 0, -1):
        for c in range(CHUNKS):
            if d == groups - 1:
                multiply(c)
            for way in ways:
                @pl.when(reaches(way, d))
                def _(way=way, d=d, c=c):
                    total = partial[c, plane + way[0] * d]
                    if d < groups - 1:
                        arrive(way, d, c)
                        total = total + way[1][d, c].astype(jnp.float32)
                    way[2][d - 1, c] = total.astype(jnp.bfloat16)
                    onward(way, d, c).start()
    for c in range(CHUNKS):
        total = partial[c, plane]
        for way in ways:
            arrive(way, 0, c)
            total = total + way[1][0, c].astype(jnp.float32)
        out_ref[:, c * chunk:(c + 1) * chunk] = total.astype(jnp.bfloat16)

    for copy in qkv:
        copy.wait_send()
    w_copy(lane).wait_send()
    for step in range(1, groups):
        spatial_copy(step).wait_send()

    @pl.when(jnp.logical_not(at_home))
    def _():
        spatial_copy(0).wait_send()

    for mine, copy in t_copies:
        @pl.when(jnp.logical_not(mine))
        def _(copy=copy):
            copy.wait_send()
    for copy in forwards:
        copy.wait_send()
    for d in range(groups - 1, 0, -1):
        for c in range(CHUNKS):
            for way in ways:
                @pl.when(reaches(way, d))
                def _(way=way, d=d, c=c):
                    onward(way, d, c).wait_send()


def kernel_body(n, groups, queries, keys, values, head_class, window_lengths, out_weight):
    tok, columns = queries.shape
    rows, out_columns = out_weight.shape
    pair, width, quarter = n // groups, tok // n, tok // groups
    chunk = out_columns // CHUNKS
    bf16, dma = jnp.bfloat16, pltpu.SemaphoreType.DMA
    line = (groups - 1, CHUNKS)
    return pl.pallas_call(
        functools.partial(layer_kernel, n, groups),
        out_shape=jax.ShapeDtypeStruct((tok, out_columns), bf16),
        in_specs=[pl.BlockSpec(memory_space=pl.ANY)] * 6,
        out_specs=pl.BlockSpec(memory_space=pltpu.VMEM),
        scratch_shapes=[
            pltpu.SMEM(head_class.shape, jnp.int32),
            pltpu.SMEM(window_lengths.shape, jnp.int32),
            pltpu.VMEM((tok, columns), bf16),
            pltpu.VMEM((tok, columns), bf16),
            pltpu.VMEM((tok, columns), bf16),
            pltpu.VMEM((n, width, 3 * TMAX * HD), bf16),
            pltpu.VMEM((n, width, 3 * TMAX * HD), bf16),
            pltpu.VMEM((groups, quarter, columns), bf16),
            pltpu.VMEM((groups, groups, quarter, columns), bf16),
            pltpu.VMEM((pair, groups, width, TMAX * HD), bf16),
            pltpu.VMEM((n, groups, width, TMAX * HD), bf16),
            pltpu.VMEM((groups, tok, columns), bf16),
            pltpu.VMEM((pair, rows, out_columns), bf16),
            pltpu.VMEM((CHUNKS, groups, tok, chunk), jnp.float32),
            pltpu.VMEM(line + (tok, chunk), bf16),
            pltpu.VMEM(line + (tok, chunk), bf16),
            pltpu.VMEM(line + (tok, chunk), bf16),
            pltpu.VMEM(line + (tok, chunk), bf16),
            dma((5,)), dma((n,)), dma((n,)),
            dma, dma, dma,
            dma((groups,)), dma((groups,)), dma((3,)), dma((groups,)),
            dma((pair, groups // 2)), dma((n,)), dma((n // 2,)),
            dma(line), dma(line), dma(line), dma(line),
        ],
        compiler_params=pltpu.CompilerParams(
            collective_id=0, has_side_effects=True, vmem_limit_bytes=VMEM_LIMIT
        ),
        cost_estimate=pl.CostEstimate(
            flops=2 * groups * tok * columns * out_columns,
            bytes_accessed=4 * rows * out_columns,
            transcendentals=local_count(columns) * tok * tok,
        ),
    )(head_class, window_lengths, queries, keys, values, out_weight)


def local_count(columns):
    return columns // HD + TMAX


def solution(mesh):
    n, groups = mesh.shape["seq"], mesh.shape["head"]

    def body(queries, keys, values, head_class, window_lengths, out_weight):
        tok, rows = queries.shape[0], out_weight.shape[0]
        if n == FRAMES and n == 2 * groups and rows > tok:
            return kernel_body(
                n, groups, queries, keys, values, head_class, window_lengths, out_weight
            )
        return gather_body(queries, keys, values, head_class, window_lengths, out_weight)

    placed = (
        P("seq", "head"),
        P("seq", "head"),
        P("seq", "head"),
        P(),
        P("seq", None),
        P("seq", "head"),
    )
    return jax.shard_map(
        body, mesh=mesh, in_specs=placed, out_specs=P("seq", "head"), check_vma=False
    )
```

```python
import functools
import math

import jax
import jax.numpy as jnp
from jax import lax
from jax.experimental import pallas as pl
from jax.experimental.pallas import tpu as pltpu
from jax.sharding import PartitionSpec as P

HD = 128
TMAX = 3
FRAMES = 8


def softmax_rows(scores):
    highest = jnp.max(scores, axis=-1, keepdims=True)
    weights = jnp.exp(scores - highest)
    return weights / jnp.sum(weights, axis=-1, keepdims=True)


def compact_heads(source, picker):
    return jnp.einsum("shd,th->std", source, picker, preferred_element_type=jnp.float32).astype(
        jnp.bfloat16
    )


def expand_heads(source, picker):
    return jnp.einsum("std,th->shd", source, picker, preferred_element_type=jnp.float32).astype(
        jnp.bfloat16
    )


def window_attention(query, key_rows, value_rows, lengths, scaling):
    ends = jnp.cumsum(lengths)
    positions = jnp.arange(query.shape[0], dtype=jnp.int32)
    window_ids = jnp.sum((positions[:, None] >= ends[None, :]).astype(jnp.int32), axis=1)
    same_window = window_ids[:, None] == window_ids[None, :]
    scores = (
        jnp.einsum("shd,thd->hst", query, key_rows, preferred_element_type=jnp.float32) * scaling
    )
    scores = jnp.where(same_window[None], scores, -1e30)
    weights = softmax_rows(scores).astype(jnp.bfloat16)
    return jnp.einsum(
        "hst,thd->shd", weights, value_rows, preferred_element_type=jnp.float32
    ).astype(jnp.bfloat16)


def gather_body(queries, keys, values, head_class, window_lengths, out_weight):
    tok_len, columns = queries.shape
    local_heads = columns // HD
    scaling = 1.0 / math.sqrt(HD)
    head_group = lax.axis_index("head")
    classes = lax.dynamic_slice_in_dim(head_class, head_group * local_heads, local_heads)
    temporal_mask = classes == 1
    slot_rank = jnp.cumsum(temporal_mask.astype(jnp.int32)) - 1
    slot_ids = jnp.arange(TMAX, dtype=jnp.int32)
    picker = ((slot_rank[None, :] == slot_ids[:, None]) & temporal_mask[None, :]).astype(
        jnp.bfloat16
    )
    shaped = [array_in.reshape(tok_len, local_heads, HD) for array_in in (queries, keys, values)]
    lengths = window_lengths[0]
    spatial_out = window_attention(shaped[0], shaped[1], shaped[2], lengths, scaling)
    packed = [compact_heads(array_in, picker)[None] for array_in in shaped]
    query = lax.all_to_all(packed[0], "seq", split_axis=1, concat_axis=0, tiled=True)
    key_rows = lax.all_to_all(packed[1], "seq", split_axis=1, concat_axis=0, tiled=True)
    value_rows = lax.all_to_all(packed[2], "seq", split_axis=1, concat_axis=0, tiled=True)
    sources, width, count, size = query.shape
    groups = sources // FRAMES
    query = query.reshape(FRAMES, groups, width, count, size)
    key_rows = key_rows.reshape(FRAMES, groups, width, count, size)
    value_rows = value_rows.reshape(FRAMES, groups, width, count, size)
    scores = (
        jnp.einsum("fjcnd,gjcnd->jcnfg", query, key_rows, preferred_element_type=jnp.float32)
        * scaling
    )
    weights = softmax_rows(scores).astype(jnp.bfloat16)
    attended = jnp.einsum(
        "jcnfg,gjcnd->fjcnd", weights, value_rows, preferred_element_type=jnp.float32
    ).astype(jnp.bfloat16)
    attended = attended.reshape(sources, width, count, size)
    returned = lax.all_to_all(attended, "seq", split_axis=0, concat_axis=1, tiled=True)
    temporal_out = expand_heads(returned[0], picker)
    mixed = jnp.where(temporal_mask[None, :, None], temporal_out, spatial_out)
    mixed_local = mixed.reshape(tok_len, local_heads * HD)
    mixed_all = lax.all_gather(mixed_local, "head", axis=1, tiled=True)
    summed = jnp.dot(
        mixed_all,
        lax.all_gather(out_weight, "seq", axis=0, tiled=True),
        preferred_element_type=jnp.float32,
    )
    return summed.astype(jnp.bfloat16)


MESH = pl.DeviceIdType.MESH
CHUNKS = 2
VMEM_LIMIT = 62 * 1024 * 1024


def masked_attention(triples, same, scaling):
    scores = [
        lax.dot_general(q, k, (((1,), (1,)), ((), ())), preferred_element_type=jnp.float32)
        for q, k, _ in triples
    ]
    scores = [jnp.where(same, score * scaling, -1e30) for score in scores]
    highest = [jnp.max(score, axis=-1, keepdims=True) for score in scores]
    weights = [jnp.exp(score - top) for score, top in zip(scores, highest)]
    totals = [jnp.sum(weight, axis=-1, keepdims=True) for weight in weights]
    weights = [(weight / total).astype(jnp.bfloat16) for weight, total in zip(weights, totals)]
    return [
        jnp.dot(weight, v, preferred_element_type=jnp.float32).astype(jnp.bfloat16)
        for weight, (_, _, v) in zip(weights, triples)
    ]


def slot_conditions(class_ref, first, local_heads):
    rank = jnp.int32(0)
    taken = []
    for h in range(local_heads):
        flag = (class_ref[first + h] == 1).astype(jnp.int32)
        taken.append([flag * (rank == t).astype(jnp.int32) == 1 for t in range(TMAX)])
        rank = rank + flag
    return taken


def layer_kernel(
    n, groups, class_hbm, len_hbm, q_hbm, k_hbm, v_hbm, w_ref, out_ref,
    class_ref, len_ref, q_ref, k_ref, v_ref,
    packed, landed, spat, spat_in, tsend, temp_in, mixed, w_all, partial,
    up_in, up_out, down_in, down_out,
    load_s, qkv_s, qkv_r, w_s, w_r, w_l, sp_s, sp_r, share_s, share_r, t_s, t_r, ts_s, ts_r,
    up_s, up_r, down_s, down_r,
):
    pair = n // groups
    seq, head = lax.axis_index("seq"), lax.axis_index("head")
    plane, lane = seq // pair, lax.rem(seq, pair)
    core = lax.rem(head, 2)
    sibling = head + 1 - 2 * core
    across = lax.rem(head + groups // 2, groups)
    tok, columns = q_ref.shape
    local_heads = columns // HD
    width, quarter = tok // n, tok // groups
    chunk = w_ref.shape[1] // CHUNKS
    rows = w_ref.shape[0]
    scaling = 1.0 / math.sqrt(HD)

    def send(src, dst, send_sem, recv_sem, to_seq, to_head):
        return pltpu.make_async_remote_copy(
            src_ref=src, dst_ref=dst, send_sem=send_sem, recv_sem=recv_sem,
            device_id=(to_seq, to_head), device_id_type=MESH,
        )

    loads = [
        pltpu.make_async_copy(src, dst, load_s.at[i])
        for i, (src, dst) in enumerate(
            ((class_hbm, class_ref), (q_hbm, q_ref), (k_hbm, k_ref), (v_hbm, v_ref), (len_hbm, len_ref))
        )
    ]
    for load in loads:
        load.start()
    own_w = pltpu.make_async_copy(w_ref, w_all.at[lane], w_l)
    own_w.start()

    barrier = pltpu.get_barrier_semaphore()

    def greet(to_seq, to_head):
        pl.semaphore_signal(barrier, inc=1, device_id=(to_seq, to_head), device_id_type=MESH)

    for step in range(1, n):
        greet(lax.rem(seq + step, n), head)
    greet(seq, sibling)
    greet(seq, across)

    @pl.when(plane != head)
    def _():
        for peer in range(n):
            greet(jnp.int32(peer), plane)

    for load in loads[:4]:
        load.wait()

    taken = slot_conditions(class_ref, head * local_heads, local_heads)
    for a, ref in enumerate((q_ref, k_ref, v_ref)):
        for t in range(TMAX):
            value = jnp.zeros((tok, HD), jnp.bfloat16)
            for h in range(t, local_heads):
                value = jnp.where(taken[h][t], ref[:, h * HD:(h + 1) * HD], value)
            at = (a * TMAX + t) * HD
            packed[:, :, at:at + HD] = value.reshape(n, width, HD)

    @pl.when(plane == 0)
    def _():
        up_in[...] = jnp.zeros_like(up_in)

    @pl.when(plane == groups - 1)
    def _():
        down_in[...] = jnp.zeros_like(down_in)

    pl.semaphore_wait(barrier, (n - 1) + pair * (groups - 1) + 2)

    qkv = []
    for step in range(1, n):
        peer = lax.rem(seq + step, n)
        copy = send(packed.at[peer], landed.at[seq], qkv_s.at[peer], qkv_r.at[seq], peer, head)
        copy.start()
        qkv.append(copy)
    landed[seq] = packed[seq]

    other = plane * pair + (1 - lane)

    def w_copy(owner):
        return send(w_ref, w_all.at[owner], w_s, w_r, other, head)

    w_copy(lane).start()

    loads[4].wait()
    def window_of(axis):
        position = lax.broadcasted_iota(jnp.int32, (tok, tok), axis)
        ids = jnp.zeros((tok, tok), jnp.int32)
        end = jnp.int32(0)
        for i in range(len_ref.shape[1]):
            end = end + len_ref[0, i]
            ids = ids + (position >= end).astype(jnp.int32)
        return ids

    same_window = window_of(0) == window_of(1)
    spans = [slice(h * HD, (h + 1) * HD) for h in range(local_heads)]
    results = masked_attention(
        [(q_ref[:, at], k_ref[:, at], v_ref[:, at]) for at in spans], same_window, scaling
    )
    for at, value in zip(spans, results):
        spat[:, :, at] = value.reshape(groups, quarter, HD)

    at_home = plane == head

    def spatial_copy(step):
        to = lax.rem(head + step, groups)
        return send(
            spat.at[to], spat_in.at[to, plane], sp_s.at[to], sp_r.at[plane], head * pair + lane, to
        )

    for step in range(1, groups):
        spatial_copy(step).start()

    @pl.when(jnp.logical_not(at_home))
    def _():
        spatial_copy(0).start()

    @pl.when(at_home)
    def _():
        spat_in[head, plane] = spat[head]

    for step in range(1, n):
        peer = lax.rem(seq + n - step, n)
        send(landed.at[peer], landed.at[peer], qkv_s.at[peer], qkv_r.at[peer], peer, head).wait_recv()
    row = lax.rem(lax.broadcasted_iota(jnp.int32, (tok, tok), 0), width)
    column = lax.rem(lax.broadcasted_iota(jnp.int32, (tok, tok), 1), width)
    same_position = row == column
    triples = [
        tuple(
            landed[:, :, (a * TMAX + t) * HD:(a * TMAX + t + 1) * HD].reshape(tok, HD)
            for a in range(3)
        )
        for t in range(TMAX)
    ]
    for t, result in enumerate(masked_attention(triples, same_position, scaling)):
        for f in range(n):
            tsend[f % pair, f // pair, :, t * HD:(t + 1) * HD] = result[f * width:(f + 1) * width]

    t_head, t_slot = lax.rem(seq, groups), seq // groups
    t_copies = []
    for x in range(pair):
        to_seq = head * pair + x
        mine = (to_seq == seq) & (t_head == head)
        copy = send(tsend.at[x], temp_in.at[t_head, t_slot], t_s.at[x], t_r.at[seq], to_seq, t_head)
        t_copies.append((mine, copy))

        @pl.when(jnp.logical_not(mine))
        def _(copy=copy):
            copy.start()

        @pl.when(mine)
        def _(x=x):
            temp_in[t_head, t_slot] = tsend[x]

    def share(which, slot, to_head):
        return send(spat_in.at[which], spat_in.at[which], share_s.at[slot], share_r.at[which], seq, to_head)

    for z in range(groups):
        @pl.when(jnp.logical_not(at_home & (plane == z)))
        def _(z=z):
            send(spat.at[z], spat_in.at[head, z], sp_s.at[z], sp_r.at[z], seq, head).wait_recv()

    share(head, 0, across).start()
    share(head, 1, sibling).start()

    def t_share(which, slot, to_head):
        return send(temp_in.at[which], temp_in.at[which], ts_s.at[slot], ts_r.at[which], seq, to_head)

    for j in range(n // groups):
        source = j * groups + head

        @pl.when(jnp.logical_not(at_home & (source == seq)))
        def _(j=j, source=source):
            send(tsend.at[0], temp_in.at[head, j], t_s.at[0], t_r.at[source], seq, head).wait_recv()

    t_share(head, 0, across).start()
    t_share(head, 1, sibling).start()

    share(across, 0, across).wait_recv()
    share(across, 2, sibling).start()
    t_share(across, 0, across).wait_recv()
    t_share(across, 2, sibling).start()
    beyond = lax.rem(sibling + groups // 2, groups)
    share(sibling, 1, sibling).wait_recv()
    share(beyond, 2, sibling).wait_recv()
    t_share(sibling, 1, sibling).wait_recv()
    t_share(beyond, 2, sibling).wait_recv()
    forwards = [share(head, 0, across), share(head, 1, sibling), share(across, 2, sibling)]
    forwards += [t_share(head, 0, across), t_share(head, 1, sibling), t_share(across, 2, sibling)]

    taken = slot_conditions(class_ref, plane * local_heads, local_heads)
    for z in range(groups):
        for h in range(local_heads):
            value = spat_in[:, z, :, h * HD:(h + 1) * HD].reshape(tok, HD)
            for t in range(min(h + 1, TMAX)):
                slot = jnp.concatenate(
                    [
                        temp_in[:, j, z, :, t * HD:(t + 1) * HD].reshape(groups * width, HD)
                        for j in range(n // groups)
                    ],
                    axis=0,
                )
                value = jnp.where(taken[h][t], slot, value)
            mixed[z, :, h * HD:(h + 1) * HD] = value

    own_w.wait()
    w_copy(1 - lane).wait_recv()

    def multiply(c):
        weight = w_all[:, :, c * chunk:(c + 1) * chunk].reshape(pair * rows, chunk)
        result = jnp.dot(
            mixed[...].reshape(groups * tok, columns), weight, preferred_element_type=jnp.float32
        )
        partial[c] = result.reshape(groups, tok, chunk)

    ways = ((1, up_in, up_out, up_s, up_r), (-1, down_in, down_out, down_s, down_r))

    def onward(way, d, c):
        sign, came, goes, s_sem, r_sem = way
        to_seq = seq + sign * pair
        return send(goes.at[d - 1, c], came.at[d - 1, c], s_sem.at[d - 1, c], r_sem.at[d - 1, c], to_seq, head)

    def has_previous(way):
        return plane > 0 if way[0] == 1 else plane < groups - 1

    def reaches(way, d):
        return plane + d < groups if way[0] == 1 else plane >= d

    def arrive(way, d, c):
        @pl.when(has_previous(way))
        def _():
            sign, came, goes, s_sem, r_sem = way
            send(goes.at[d, c], came.at[d, c], s_sem.at[d, c], r_sem.at[d, c], seq, head).wait_recv()

    for d in range(groups - 1, 0, -1):
        for c in range(CHUNKS):
            if d == groups - 1:
                multiply(c)
            for way in ways:
                @pl.when(reaches(way, d))
                def _(way=way, d=d, c=c):
                    total = partial[c, plane + way[0] * d]
                    if d < groups - 1:
                        arrive(way, d, c)
                        total = total + way[1][d, c].astype(jnp.float32)
                    way[2][d - 1, c] = total.astype(jnp.bfloat16)
                    onward(way, d, c).start()
    for c in range(CHUNKS):
        total = partial[c, plane]
        for way in ways:
            arrive(way, 0, c)
            total = total + way[1][0, c].astype(jnp.float32)
        out_ref[:, c * chunk:(c + 1) * chunk] = total.astype(jnp.bfloat16)

    for copy in qkv:
        copy.wait_send()
    w_copy(lane).wait_send()
    for step in range(1, groups):
        spatial_copy(step).wait_send()

    @pl.when(jnp.logical_not(at_home))
    def _():
        spatial_copy(0).wait_send()

    for mine, copy in t_copies:
        @pl.when(jnp.logical_not(mine))
        def _(copy=copy):
            copy.wait_send()
    for copy in forwards:
        copy.wait_send()
    for d in range(groups - 1, 0, -1):
        for c in range(CHUNKS):
            for way in ways:
                @pl.when(reaches(way, d))
                def _(way=way, d=d, c=c):
                    onward(way, d, c).wait_send()


def kernel_body(n, groups, queries, keys, values, head_class, window_lengths, out_weight):
    tok, columns = queries.shape
    rows, out_columns = out_weight.shape
    pair, width, quarter = n // groups, tok // n, tok // groups
    chunk = out_columns // CHUNKS
    bf16, dma = jnp.bfloat16, pltpu.SemaphoreType.DMA
    line = (groups - 1, CHUNKS)
    return pl.pallas_call(
        functools.partial(layer_kernel, n, groups),
        out_shape=jax.ShapeDtypeStruct((tok, out_columns), bf16),
        in_specs=[pl.BlockSpec(memory_space=pl.ANY)] * 6,
        out_specs=pl.BlockSpec(memory_space=pltpu.VMEM),
        scratch_shapes=[
            pltpu.SMEM(head_class.shape, jnp.int32),
            pltpu.SMEM(window_lengths.shape, jnp.int32),
            pltpu.VMEM((tok, columns), bf16),
            pltpu.VMEM((tok, columns), bf16),
            pltpu.VMEM((tok, columns), bf16),
            pltpu.VMEM((n, width, 3 * TMAX * HD), bf16),
            pltpu.VMEM((n, width, 3 * TMAX * HD), bf16),
            pltpu.VMEM((groups, quarter, columns), bf16),
            pltpu.VMEM((groups, groups, quarter, columns), bf16),
            pltpu.VMEM((pair, groups, width, TMAX * HD), bf16),
            pltpu.VMEM((groups, n // groups, groups, width, TMAX * HD), bf16),
            pltpu.VMEM((groups, tok, columns), bf16),
            pltpu.VMEM((pair, rows, out_columns), bf16),
            pltpu.VMEM((CHUNKS, groups, tok, chunk), jnp.float32),
            pltpu.VMEM(line + (tok, chunk), bf16),
            pltpu.VMEM(line + (tok, chunk), bf16),
            pltpu.VMEM(line + (tok, chunk), bf16),
            pltpu.VMEM(line + (tok, chunk), bf16),
            dma((5,)), dma((n,)), dma((n,)),
            dma, dma, dma,
            dma((groups,)), dma((groups,)), dma((3,)), dma((groups,)),
            dma((pair,)), dma((n,)), dma((3,)), dma((groups,)),
            dma(line), dma(line), dma(line), dma(line),
        ],
        compiler_params=pltpu.CompilerParams(
            collective_id=0, has_side_effects=True, vmem_limit_bytes=VMEM_LIMIT
        ),
        cost_estimate=pl.CostEstimate(
            flops=2 * groups * tok * columns * out_columns,
            bytes_accessed=4 * rows * out_columns,
            transcendentals=local_count(columns) * tok * tok,
        ),
    )(head_class, window_lengths, queries, keys, values, out_weight)


def local_count(columns):
    return columns // HD + TMAX


def solution(mesh):
    n, groups = mesh.shape["seq"], mesh.shape["head"]

    def body(queries, keys, values, head_class, window_lengths, out_weight):
        tok, rows = queries.shape[0], out_weight.shape[0]
        if n == FRAMES and n == 2 * groups and rows > tok:
            return kernel_body(
                n, groups, queries, keys, values, head_class, window_lengths, out_weight
            )
        return gather_body(queries, keys, values, head_class, window_lengths, out_weight)

    placed = (
        P("seq", "head"),
        P("seq", "head"),
        P("seq", "head"),
        P(),
        P("seq", None),
        P("seq", "head"),
    )
    return jax.shard_map(
        body, mesh=mesh, in_specs=placed, out_specs=P("seq", "head"), check_vma=False
    )
```

```python
import functools
import math

import jax
import jax.numpy as jnp
from jax import lax
from jax.experimental import pallas as pl
from jax.experimental.pallas import tpu as pltpu
from jax.sharding import PartitionSpec as P

HD = 128
TMAX = 3
FRAMES = 8


def softmax_rows(scores):
    highest = jnp.max(scores, axis=-1, keepdims=True)
    weights = jnp.exp(scores - highest)
    return weights / jnp.sum(weights, axis=-1, keepdims=True)


def compact_heads(source, picker):
    return jnp.einsum("shd,th->std", source, picker, preferred_element_type=jnp.float32).astype(
        jnp.bfloat16
    )


def expand_heads(source, picker):
    return jnp.einsum("std,th->shd", source, picker, preferred_element_type=jnp.float32).astype(
        jnp.bfloat16
    )


def window_attention(query, key_rows, value_rows, lengths, scaling):
    ends = jnp.cumsum(lengths)
    positions = jnp.arange(query.shape[0], dtype=jnp.int32)
    window_ids = jnp.sum((positions[:, None] >= ends[None, :]).astype(jnp.int32), axis=1)
    same_window = window_ids[:, None] == window_ids[None, :]
    scores = (
        jnp.einsum("shd,thd->hst", query, key_rows, preferred_element_type=jnp.float32) * scaling
    )
    scores = jnp.where(same_window[None], scores, -1e30)
    weights = softmax_rows(scores).astype(jnp.bfloat16)
    return jnp.einsum(
        "hst,thd->shd", weights, value_rows, preferred_element_type=jnp.float32
    ).astype(jnp.bfloat16)


def gather_body(queries, keys, values, head_class, window_lengths, out_weight):
    tok_len, columns = queries.shape
    local_heads = columns // HD
    scaling = 1.0 / math.sqrt(HD)
    head_group = lax.axis_index("head")
    classes = lax.dynamic_slice_in_dim(head_class, head_group * local_heads, local_heads)
    temporal_mask = classes == 1
    slot_rank = jnp.cumsum(temporal_mask.astype(jnp.int32)) - 1
    slot_ids = jnp.arange(TMAX, dtype=jnp.int32)
    picker = ((slot_rank[None, :] == slot_ids[:, None]) & temporal_mask[None, :]).astype(
        jnp.bfloat16
    )
    shaped = [array_in.reshape(tok_len, local_heads, HD) for array_in in (queries, keys, values)]
    lengths = window_lengths[0]
    spatial_out = window_attention(shaped[0], shaped[1], shaped[2], lengths, scaling)
    packed = [compact_heads(array_in, picker)[None] for array_in in shaped]
    query = lax.all_to_all(packed[0], "seq", split_axis=1, concat_axis=0, tiled=True)
    key_rows = lax.all_to_all(packed[1], "seq", split_axis=1, concat_axis=0, tiled=True)
    value_rows = lax.all_to_all(packed[2], "seq", split_axis=1, concat_axis=0, tiled=True)
    sources, width, count, size = query.shape
    groups = sources // FRAMES
    query = query.reshape(FRAMES, groups, width, count, size)
    key_rows = key_rows.reshape(FRAMES, groups, width, count, size)
    value_rows = value_rows.reshape(FRAMES, groups, width, count, size)
    scores = (
        jnp.einsum("fjcnd,gjcnd->jcnfg", query, key_rows, preferred_element_type=jnp.float32)
        * scaling
    )
    weights = softmax_rows(scores).astype(jnp.bfloat16)
    attended = jnp.einsum(
        "jcnfg,gjcnd->fjcnd", weights, value_rows, preferred_element_type=jnp.float32
    ).astype(jnp.bfloat16)
    attended = attended.reshape(sources, width, count, size)
    returned = lax.all_to_all(attended, "seq", split_axis=0, concat_axis=1, tiled=True)
    temporal_out = expand_heads(returned[0], picker)
    mixed = jnp.where(temporal_mask[None, :, None], temporal_out, spatial_out)
    mixed_local = mixed.reshape(tok_len, local_heads * HD)
    mixed_all = lax.all_gather(mixed_local, "head", axis=1, tiled=True)
    summed = jnp.dot(
        mixed_all,
        lax.all_gather(out_weight, "seq", axis=0, tiled=True),
        preferred_element_type=jnp.float32,
    )
    return summed.astype(jnp.bfloat16)


MESH = pl.DeviceIdType.MESH
CHUNKS = 2
VMEM_LIMIT = 62 * 1024 * 1024


def masked_attention(triples, same, scaling):
    scores = [
        lax.dot_general(q, k, (((1,), (1,)), ((), ())), preferred_element_type=jnp.float32)
        for q, k, _ in triples
    ]
    scores = [jnp.where(same, score * scaling, -1e30) for score in scores]
    highest = [jnp.max(score, axis=-1, keepdims=True) for score in scores]
    weights = [jnp.exp(score - top) for score, top in zip(scores, highest)]
    totals = [jnp.sum(weight, axis=-1, keepdims=True) for weight in weights]
    weights = [(weight / total).astype(jnp.bfloat16) for weight, total in zip(weights, totals)]
    return [
        jnp.dot(weight, v, preferred_element_type=jnp.float32).astype(jnp.bfloat16)
        for weight, (_, _, v) in zip(weights, triples)
    ]


def slot_conditions(class_ref, first, local_heads, wanted, slots):
    rank = jnp.int32(0)
    taken = []
    for h in range(local_heads):
        flag = (class_ref[first + h] == wanted).astype(jnp.int32)
        taken.append([flag * (rank == t).astype(jnp.int32) == 1 for t in range(slots)])
        rank = rank + flag
    return taken


def layer_kernel(
    n, groups, class_hbm, len_hbm, q_hbm, k_hbm, v_hbm, w_ref, out_ref,
    class_ref, len_ref, q_ref, k_ref, v_ref,
    packed, landed, spat, spat_in, tsend, temp_in, mixed, w_all, partial,
    up_in, up_out, down_in, down_out,
    load_s, qkv_s, qkv_r, w_s, w_r, w_l, sp_s, sp_r, share_s, share_r, t_s, t_r, tf_s,
    up_s, up_r, down_s, down_r,
):
    pair = n // groups
    seq, head = lax.axis_index("seq"), lax.axis_index("head")
    plane, lane = seq // pair, lax.rem(seq, pair)
    core = lax.rem(head, 2)
    sibling = head + 1 - 2 * core
    across = lax.rem(head + groups // 2, groups)
    tok, columns = q_ref.shape
    local_heads = columns // HD
    width, quarter = tok // n, tok // groups
    spatial_slots = local_heads - 1
    chunk = w_ref.shape[1] // CHUNKS
    rows = w_ref.shape[0]
    scaling = 1.0 / math.sqrt(HD)

    def send(src, dst, send_sem, recv_sem, to_seq, to_head):
        return pltpu.make_async_remote_copy(
            src_ref=src, dst_ref=dst, send_sem=send_sem, recv_sem=recv_sem,
            device_id=(to_seq, to_head), device_id_type=MESH,
        )

    loads = [
        pltpu.make_async_copy(src, dst, load_s.at[i])
        for i, (src, dst) in enumerate(
            ((class_hbm, class_ref), (q_hbm, q_ref), (k_hbm, k_ref), (v_hbm, v_ref), (len_hbm, len_ref))
        )
    ]
    for load in loads:
        load.start()
    own_w = pltpu.make_async_copy(w_ref, w_all.at[lane], w_l)
    own_w.start()

    barrier = pltpu.get_barrier_semaphore()

    def greet(to_seq, to_head):
        pl.semaphore_signal(barrier, inc=1, device_id=(to_seq, to_head), device_id_type=MESH)

    for step in range(1, n):
        greet(lax.rem(seq + step, n), head)
    greet(seq, sibling)
    greet(seq, across)

    @pl.when(plane != head)
    def _():
        for peer in range(n):
            greet(jnp.int32(peer), plane)

    for load in loads[:4]:
        load.wait()

    taken = slot_conditions(class_ref, head * local_heads, local_heads, 1, TMAX)
    for a, ref in enumerate((q_ref, k_ref, v_ref)):
        for t in range(TMAX):
            value = jnp.zeros((tok, HD), jnp.bfloat16)
            for h in range(t, local_heads):
                value = jnp.where(taken[h][t], ref[:, h * HD:(h + 1) * HD], value)
            at = (a * TMAX + t) * HD
            packed[:, :, at:at + HD] = value.reshape(n, width, HD)

    @pl.when(plane == 0)
    def _():
        up_in[...] = jnp.zeros_like(up_in)

    @pl.when(plane == groups - 1)
    def _():
        down_in[...] = jnp.zeros_like(down_in)

    pl.semaphore_wait(barrier, (n - 1) + pair * (groups - 1) + 2)

    qkv = []
    for step in range(1, n):
        peer = lax.rem(seq + step, n)
        copy = send(packed.at[peer], landed.at[seq], qkv_s.at[peer], qkv_r.at[seq], peer, head)
        copy.start()
        qkv.append(copy)
    landed[seq] = packed[seq]

    other = plane * pair + (1 - lane)

    def w_copy(owner):
        return send(w_ref, w_all.at[owner], w_s, w_r, other, head)

    w_copy(lane).start()

    loads[4].wait()
    def window_of(axis):
        position = lax.broadcasted_iota(jnp.int32, (tok, tok), axis)
        ids = jnp.zeros((tok, tok), jnp.int32)
        end = jnp.int32(0)
        for i in range(len_ref.shape[1]):
            end = end + len_ref[0, i]
            ids = ids + (position >= end).astype(jnp.int32)
        return ids

    same_window = window_of(0) == window_of(1)
    spans = [slice(h * HD, (h + 1) * HD) for h in range(local_heads)]
    results = masked_attention(
        [(q_ref[:, at], k_ref[:, at], v_ref[:, at]) for at in spans], same_window, scaling
    )
    others = slot_conditions(class_ref, head * local_heads, local_heads, 0, spatial_slots)
    for u in range(spatial_slots):
        value = jnp.zeros((tok, HD), jnp.bfloat16)
        for h in range(u, local_heads):
            value = jnp.where(others[h][u], results[h], value)
        spat[:, :, spans[u]] = value.reshape(groups, quarter, HD)

    at_home = plane == head

    def spatial_copy(step):
        to = lax.rem(head + step, groups)
        return send(
            spat.at[to], spat_in.at[to, plane], sp_s.at[to], sp_r.at[plane], head * pair + lane, to
        )

    for step in range(1, groups):
        spatial_copy(step).start()

    @pl.when(jnp.logical_not(at_home))
    def _():
        spatial_copy(0).start()

    @pl.when(at_home)
    def _():
        spat_in[head, plane] = spat[head]

    for step in range(1, n):
        peer = lax.rem(seq + n - step, n)
        send(landed.at[peer], landed.at[peer], qkv_s.at[peer], qkv_r.at[peer], peer, head).wait_recv()
    row = lax.rem(lax.broadcasted_iota(jnp.int32, (tok, tok), 0), width)
    column = lax.rem(lax.broadcasted_iota(jnp.int32, (tok, tok), 1), width)
    same_position = row == column
    triples = [
        tuple(
            landed[:, :, (a * TMAX + t) * HD:(a * TMAX + t + 1) * HD].reshape(tok, HD)
            for a in range(3)
        )
        for t in range(TMAX)
    ]
    for t, result in enumerate(masked_attention(triples, same_position, scaling)):
        for f in range(n):
            tsend[f % pair, f // pair, :, t * HD:(t + 1) * HD] = result[f * width:(f + 1) * width]

    t_core = lax.rem(seq, 2)
    t_copies = []
    for x in range(pair):
        for y in range(groups // 2):
            to_seq, to_head = head * pair + x, 2 * y + t_core
            mine = (to_seq == seq) & (to_head == head)
            copy = send(tsend.at[x], temp_in.at[seq], t_s.at[x, y], t_r.at[seq], to_seq, to_head)
            t_copies.append((mine, copy))

            @pl.when(jnp.logical_not(mine))
            def _(copy=copy):
                copy.start()

            @pl.when(mine)
            def _(x=x):
                temp_in[seq] = tsend[x]

    def share(which, slot, to_head):
        return send(spat_in.at[which], spat_in.at[which], share_s.at[slot], share_r.at[which], seq, to_head)

    for z in range(groups):
        @pl.when(jnp.logical_not(at_home & (plane == z)))
        def _(z=z):
            send(spat.at[z], spat_in.at[head, z], sp_s.at[z], sp_r.at[z], seq, head).wait_recv()

    share(head, 0, across).start()
    share(head, 1, sibling).start()

    forwards = [share(head, 0, across), share(head, 1, sibling), share(across, 2, sibling)]
    for j in range(n // 2):
        source = 2 * j + core
        here = (source == seq) & (plane == head)
        copy = send(temp_in.at[source], temp_in.at[source], tf_s.at[j], t_r.at[source], seq, sibling)

        @pl.when(jnp.logical_not(here))
        def _(copy=copy):
            copy.wait_recv()

        copy.start()
        forwards.append(copy)
    share(across, 0, across).wait_recv()
    share(across, 2, sibling).start()
    share(sibling, 1, sibling).wait_recv()
    share(lax.rem(sibling + groups // 2, groups), 2, sibling).wait_recv()
    for j in range(n // 2):
        source = 2 * j + 1 - core
        send(temp_in.at[source], temp_in.at[source], tf_s.at[j], t_r.at[source], seq, sibling).wait_recv()

    taken = slot_conditions(class_ref, plane * local_heads, local_heads, 1, TMAX)
    others = slot_conditions(class_ref, plane * local_heads, local_heads, 0, spatial_slots)
    for z in range(groups):
        for h in range(local_heads):
            value = jnp.zeros((tok, HD), jnp.bfloat16)
            for u in range(min(h + 1, spatial_slots)):
                slot = spat_in[:, z, :, u * HD:(u + 1) * HD].reshape(tok, HD)
                value = jnp.where(others[h][u], slot, value)
            for t in range(min(h + 1, TMAX)):
                slot = temp_in[:, z, :, t * HD:(t + 1) * HD].reshape(tok, HD)
                value = jnp.where(taken[h][t], slot, value)
            mixed[z, :, h * HD:(h + 1) * HD] = value

    own_w.wait()
    w_copy(1 - lane).wait_recv()

    def multiply(c):
        weight = w_all[:, :, c * chunk:(c + 1) * chunk].reshape(pair * rows, chunk)
        result = jnp.dot(
            mixed[...].reshape(groups * tok, columns), weight, preferred_element_type=jnp.float32
        )
        partial[c] = result.reshape(groups, tok, chunk)

    ways = ((1, up_in, up_out, up_s, up_r), (-1, down_in, down_out, down_s, down_r))

    def onward(way, d, c):
        sign, came, goes, s_sem, r_sem = way
        to_seq = seq + sign * pair
        return send(goes.at[d - 1, c], came.at[d - 1, c], s_sem.at[d - 1, c], r_sem.at[d - 1, c], to_seq, head)

    def has_previous(way):
        return plane > 0 if way[0] == 1 else plane < groups - 1

    def reaches(way, d):
        return plane + d < groups if way[0] == 1 else plane >= d

    def arrive(way, d, c):
        @pl.when(has_previous(way))
        def _():
            sign, came, goes, s_sem, r_sem = way
            send(goes.at[d, c], came.at[d, c], s_sem.at[d, c], r_sem.at[d, c], seq, head).wait_recv()

    for d in range(groups - 1, 0, -1):
        for c in range(CHUNKS):
            if d == groups - 1:
                multiply(c)
            for way in ways:
                @pl.when(reaches(way, d))
                def _(way=way, d=d, c=c):
                    total = partial[c, plane + way[0] * d]
                    if d < groups - 1:
                        arrive(way, d, c)
                        total = total + way[1][d, c].astype(jnp.float32)
                    way[2][d - 1, c] = total.astype(jnp.bfloat16)
                    onward(way, d, c).start()
    for c in range(CHUNKS):
        total = partial[c, plane]
        for way in ways:
            arrive(way, 0, c)
            total = total + way[1][0, c].astype(jnp.float32)
        out_ref[:, c * chunk:(c + 1) * chunk] = total

    for copy in qkv:
        copy.wait_send()
    w_copy(lane).wait_send()
    for step in range(1, groups):
        spatial_copy(step).wait_send()

    @pl.when(jnp.logical_not(at_home))
    def _():
        spatial_copy(0).wait_send()

    for mine, copy in t_copies:
        @pl.when(jnp.logical_not(mine))
        def _(copy=copy):
            copy.wait_send()
    for copy in forwards:
        copy.wait_send()
    for d in range(groups - 1, 0, -1):
        for c in range(CHUNKS):
            for way in ways:
                @pl.when(reaches(way, d))
                def _(way=way, d=d, c=c):
                    onward(way, d, c).wait_send()


def kernel_body(n, groups, queries, keys, values, head_class, window_lengths, out_weight):
    tok, columns = queries.shape
    rows, out_columns = out_weight.shape
    pair, width, quarter = n // groups, tok // n, tok // groups
    chunk = out_columns // CHUNKS
    bf16, dma = jnp.bfloat16, pltpu.SemaphoreType.DMA
    line = (groups - 1, CHUNKS)
    return pl.pallas_call(
        functools.partial(layer_kernel, n, groups),
        out_shape=jax.ShapeDtypeStruct((tok, out_columns), jnp.float32),
        in_specs=[pl.BlockSpec(memory_space=pl.ANY)] * 6,
        out_specs=pl.BlockSpec(memory_space=pltpu.VMEM),
        scratch_shapes=[
            pltpu.SMEM(head_class.shape, jnp.int32),
            pltpu.SMEM(window_lengths.shape, jnp.int32),
            pltpu.VMEM((tok, columns), bf16),
            pltpu.VMEM((tok, columns), bf16),
            pltpu.VMEM((tok, columns), bf16),
            pltpu.VMEM((n, width, 3 * TMAX * HD), bf16),
            pltpu.VMEM((n, width, 3 * TMAX * HD), bf16),
            pltpu.VMEM((groups, quarter, columns - HD), bf16),
            pltpu.VMEM((groups, groups, quarter, columns - HD), bf16),
            pltpu.VMEM((pair, groups, width, TMAX * HD), bf16),
            pltpu.VMEM((n, groups, width, TMAX * HD), bf16),
            pltpu.VMEM((groups, tok, columns), bf16),
            pltpu.VMEM((pair, rows, out_columns), bf16),
            pltpu.VMEM((CHUNKS, groups, tok, chunk), jnp.float32),
            pltpu.VMEM(line + (tok, chunk), bf16),
            pltpu.VMEM(line + (tok, chunk), bf16),
            pltpu.VMEM(line + (tok, chunk), bf16),
            pltpu.VMEM(line + (tok, chunk), bf16),
            dma((5,)), dma((n,)), dma((n,)),
            dma, dma, dma,
            dma((groups,)), dma((groups,)), dma((3,)), dma((groups,)),
            dma((pair, groups // 2)), dma((n,)), dma((n // 2,)),
            dma(line), dma(line), dma(line), dma(line),
        ],
        compiler_params=pltpu.CompilerParams(
            collective_id=0, has_side_effects=True, vmem_limit_bytes=VMEM_LIMIT
        ),
        cost_estimate=pl.CostEstimate(
            flops=2 * groups * tok * columns * out_columns,
            bytes_accessed=4 * rows * out_columns,
            transcendentals=local_count(columns) * tok * tok,
        ),
    )(head_class, window_lengths, queries, keys, values, out_weight).astype(bf16)


def local_count(columns):
    return columns // HD + TMAX


def solution(mesh):
    n, groups = mesh.shape["seq"], mesh.shape["head"]

    def body(queries, keys, values, head_class, window_lengths, out_weight):
        tok, rows = queries.shape[0], out_weight.shape[0]
        if n == FRAMES and n == 2 * groups and rows > tok:
            return kernel_body(
                n, groups, queries, keys, values, head_class, window_lengths, out_weight
            )
        return gather_body(queries, keys, values, head_class, window_lengths, out_weight)

    placed = (
        P("seq", "head"),
        P("seq", "head"),
        P("seq", "head"),
        P(),
        P("seq", None),
        P("seq", "head"),
    )
    return jax.shard_map(
        body, mesh=mesh, in_specs=placed, out_specs=P("seq", "head"), check_vma=False
    )
```
